512 devices in a mesh: basis: 32 (over z_hi, x, core), query: 16 (over z_lo, y).
Axes of the slice: x: 4, y: 4, z: 16 (z_hi: 4, z_lo: 4; z = z_hi * 4 + z_lo), core: 2. Of those that a mesh axis runs over, the one named last changes fastest.
Arguments:
- train_inputs: bfloat16 [256, 8192], P(None, 'basis'), may hold values from -6 to 6
- train_grads: bfloat16 [256, 8192], P(None, 'query'), may hold values from -0.375 to 0.375
- example_ids: int32 [256], replicated, may hold values from 0 to 3, never falling along the last dimension, each value on 1 to 128 neighbouring positions
- task_ids: int32 [48, 1], replicated, may hold values from 0 to 15
- basis_in: bfloat16 [8192, 8192], P('basis', 'query'), may hold values from -0.0625 to 0.0625
- basis_out: bfloat16 [8192, 8192], P('query', 'basis'), may hold values from -0.0625 to 0.0625
- eigenvalues: float32 [8192, 8192], P('basis', 'query'), may hold values from 0.2 to 5
- query_in: bfloat16 [8192, 1536], P('basis'), may hold values from -0.0625 to 0.0625
- query_out: bfloat16 [8192, 1536], P('query'), may hold values from -0.0625 to 0.0625
Outputs:
- precond_total: bfloat16 [8192, 8192], P('basis', 'query')
- influence: float32 [4, 48], replicated
- task_influence: float32 [4, 16], replicated
The draws below stay inside these ranges and needn't reach their ends.
Inputs may be any that keep to these rules, and one draw needn't show every extreme that they name: `example_ids`: example ids never fall along the rows; each example has 1 to 128 rows. `task_ids`: each task has one query or more.
All inputs are finite; a program needn't handle non-finite values.
Results may differ from the reference program's by a relative error of at most 0.0013.
Values sent between devices are 32-bit elements; how exact they have to be, the bound alone decides.
A program may use at most 64 MiB of HBM per device.

```python
import math
import jax
import jax.numpy as jnp
import numpy as np
from jax import lax

D = 8192
TOKENS = 256
EXAMPLES = 4
QUERIES = 48
TASKS = 16
RANK = 32
QC = 1536


def level_of(stream_key, extent, shards, low, high):
    level, own = 1.0, jax.random.fold_in(stream_key, 6)
    for position, shards_of in shards:
        heights = jnp.exp(jax.random.uniform(jax.random.fold_in(own, position), (shards_of,), jnp.float32, low / len(shards), high / len(shards)))
        level = level * jnp.repeat(heights, extent[position] // shards_of).reshape([-1 if axis == position else 1 for axis in range(len(extent))])
    return level


def picks_of(key, rows, count, top, lift):
    order = jax.random.permutation(jax.random.fold_in(key, 1), count)
    pull = order
    for power in range(3):
        pull = pull * pull // count
    pull = pull * lift // count
    tickets = jax.random.randint(jax.random.fold_in(key, 2), (rows, count), 0, 4096) + pull
    sure = jax.random.permutation(jax.random.fold_in(key, 3), rows)[jnp.arange(count) % rows]
    tickets = jnp.where(jnp.arange(rows)[:, None] == sure[None, :], 1 << 14, tickets)
    score = tickets * count + jnp.arange(count)
    return lax.top_k(score.astype(jnp.int32), top)[1].astype(jnp.int32)


def split_up(amount, total, bound, lean):
    weights = [(1 << 20) // math.isqrt(rank ** lean) + 1 for rank in range(2, amount + 1)]
    rest, holding = total - bound - (amount - 1), [1] * (amount - 1)
    while rest > 0:
        free = [i for i in range(amount - 1) if holding[i] < bound]
        pool, left = sum([weights[i] for i in free]), rest
        for i in free:
            addition = min(bound - holding[i], max(1, left * weights[i] // pool), rest)
            holding[i] = holding[i] + addition
            rest = rest - addition
    return np.array([bound] + holding)


def uneven(own_key, amount, total, most, lean):
    if amount == 2:
        one = jax.random.randint(own_key, (), max(1, total - most), min(most, total - 1) + 1)
        return jnp.stack([one, total - one])
    lengths = jnp.asarray(split_up(amount, total, most, lean), jnp.int32)
    twos = (amount - 1) // 2
    giver, receiver = lengths[1:1 + 2 * twos:2], lengths[2:2 + 2 * twos:2]
    slack = jnp.minimum(giver - 1, most - receiver)
    passed = jax.random.randint(jax.random.fold_in(own_key, 1), (twos,), 0, 1 << 20) % (slack + 1)
    lengths = lengths.at[1:1 + 2 * twos:2].set(giver - passed).at[2:2 + 2 * twos:2].set(receiver + passed)
    return lengths[jax.random.permutation(jax.random.fold_in(own_key, 2), amount)]


def gaussian(stream_key, shape, spread, reach, cuts=(), held_as=jnp.bfloat16):
    drawn = spread * jax.random.normal(stream_key, shape, jnp.float32)
    if cuts:
        drawn = drawn * level_of(stream_key, shape, cuts, -0.22, 0.18)
    return jnp.clip(drawn, -reach, reach).astype(held_as)


def setup_inputs(seed: int = 0) -> dict:
    key_of = jax.random.split(jax.random.key(seed), 10)
    return {
        "train_inputs": gaussian(key_of[0], (TOKENS, D), 1.0, 6.0, ((1, 32),)),
        "train_grads": gaussian(key_of[1], (TOKENS, D), TOKENS ** -0.5, 0.375, ((1, 16),)),
        "example_ids": jnp.searchsorted(jnp.cumsum(uneven(key_of[2], EXAMPLES, TOKENS, TOKENS // 2, 0)), jnp.arange(TOKENS), side="right").astype(jnp.int32),
        "task_ids": picks_of(key_of[3], QUERIES, TASKS, 1, 512),
        "basis_in": gaussian(key_of[4], (D, D), D ** -0.5, 0.0625, ((0, 32), (1, 16))),
        "basis_out": gaussian(key_of[5], (D, D), D ** -0.5, 0.0625, ((0, 16), (1, 32))),
        "eigenvalues": jnp.clip(jnp.exp(math.log(5.0) - 3.218876 * jax.random.uniform(key_of[6], (D, D), jnp.float32) ** level_of(key_of[6], (D, D), ((0, 32), (1, 16)), -0.2, 0.2)), 0.2, 5.0),
        "query_in": gaussian(key_of[7], (D, QC), D ** -0.5, 0.0625, ((0, 32),)),
        "query_out": gaussian(key_of[8], (D, QC), D ** -0.5, 0.0625, ((0, 16),)),
    }


DAMPING = 0.05


def reference(train_inputs, train_grads, example_ids, task_ids, basis_in, basis_out, eigenvalues, query_in, query_out):
    rot_grads = jnp.dot(train_grads, basis_out, preferred_element_type=jnp.float32)
    rot_inputs = jnp.dot(train_inputs, basis_in, preferred_element_type=jnp.float32)
    rot_query_out = jnp.dot(basis_out.T, query_out, preferred_element_type=jnp.float32)
    rot_query_in = jnp.dot(basis_in.T, query_in, preferred_element_type=jnp.float32)
    block_width = min(D, 1024)
    block_count = D // block_width
    one_hot = example_ids[None, :] == jnp.arange(EXAMPLES, dtype=jnp.int32)[:, None]
    grad_blocks = rot_grads.reshape(TOKENS, block_count, block_width).transpose(1, 0, 2)
    eigen_blocks = eigenvalues.reshape(block_count, block_width, D)
    out_blocks = rot_query_out.reshape(block_count, block_width, QC)

    def one_block(block_items):
        grad_part, eigen_part, out_part = block_items
        selected = jnp.where(one_hot[:, :, None], grad_part[None], jnp.zeros((), grad_part.dtype))
        scaled = jnp.einsum("nti,tj->nij", selected, rot_inputs, precision=lax.Precision.HIGHEST) / (eigen_part + DAMPING)[None]
        summed = jnp.sum(scaled, axis=0).astype(jnp.bfloat16)
        weighted = jnp.einsum("nij,jc->nic", scaled, rot_query_in, precision=lax.Precision.HIGHEST)
        partial_value = jnp.sum(weighted * out_part[None], axis=1)
        return summed, partial_value

    summed_blocks, partials = lax.map(one_block, (grad_blocks, eigen_blocks, out_blocks))
    precond_total = summed_blocks.reshape(D, D)
    influence = jnp.sum(partials, axis=0).reshape(EXAMPLES, QUERIES, RANK).sum(axis=2)
    task_table = (task_ids == jnp.arange(TASKS, dtype=jnp.int32)[None, :]).astype(jnp.float32)
    counts = jnp.sum(task_table, axis=0)
    task_influence = jnp.dot(influence, task_table, precision=lax.Precision.HIGHEST) / counts[None, :]
    return precond_total, influence, task_influence
```

```python
import functools

import jax
import jax.numpy as jnp
from jax import lax
from jax.experimental import pallas as pl
from jax.experimental.pallas import tpu as pltpu
from jax.sharding import PartitionSpec as P

EXAMPLES = 4
QUERIES = 48
TASKS = 16
RANK = 32
DAMPING = 0.05
TOKENS = 256
QC = QUERIES * RANK
JB = 512
IB = 256
LANES = 128

WIDTHS = (256, 512, 512, 512)
STARTS = tuple(sum(WIDTHS[:s]) for s in range(len(WIDTHS)))
STAGES = len(WIDTHS)
TOTAL = sum(WIDTHS)
MESH = pl.DeviceIdType.MESH
COPIES = 160


def dot(a, b, contract=((1,), (0,))):
    return lax.dot_general(a, b, (contract, ((), ())), preferred_element_type=jnp.float32)


def split(value):
    high = value.astype(jnp.bfloat16)
    return high, (value - high.astype(jnp.float32)).astype(jnp.bfloat16)


def select_dot(value, table):
    high, rest = split(value)
    mid = (value - high.astype(jnp.float32) - rest.astype(jnp.float32)).astype(jnp.bfloat16)
    return dot(high, table) + dot(rest, table) + dot(mid, table)


def kernel(
    h_tin, h_tgr, h_eid, h_tid, h_bin, h_bout, h_eig, h_qin, h_qout,
    o_total, o_inf, o_task,
    tin, tgr, eid, tid, b_in, b_out, eig, qin, qout,
    bt_in, bt_out, inv,
    pb, fb, ls, lx, lz, lw, cz, pq, fq, ly, le, li,
    s_hi, s_lo, part, ar_c, ar_x, ar_y, ar_l, ar_h,
    send_sem, recv_sem, load_sem,
):
    basis, query = lax.axis_index("basis"), lax.axis_index("query")
    zh, x, core = basis // 8, (basis // 2) % 4, basis % 2
    zl, y = query // 4, query % 4

    def dev(zh=zh, x=x, core=core, zl=zl, y=y):
        return (zh * 8 + x * 2 + core, zl * 4 + y)

    sibling = dev(core=1 - core)
    xs = [None] + [dev(x=(x + d) % 4) for d in (1, 2, 3)]
    ys = [None] + [dev(y=(y + d) % 4) for d in (1, 2, 3)]
    zhs = [None] + [dev(zh=(zh + d) % 4) for d in (1, 2, 3)]
    zls = [None] + [dev(zl=(zl + d) % 4) for d in (1, 2, 3)]

    loads = []
    for n, (src, dst) in enumerate((
        (h_bin, b_in), (h_tin, tin), (h_bout, b_out), (h_tgr, tgr), (h_qin, qin),
        (h_qout, qout), (h_eig, eig), (h_eid, eid), (h_tid, tid),
    )):
        load = pltpu.make_async_copy(src, dst, load_sem.at[n])
        load.start()
        loads.append(load)

    barrier = pltpu.get_barrier_semaphore()
    peers = [sibling] + xs[1:] + ys[1:] + zhs[1:] + zls[1:]
    for peer in peers:
        pl.semaphore_signal(barrier, inc=1, device_id=peer, device_id_type=MESH)

    made = [0]

    def copy(src, dst, target):
        n = made[0]
        made[0] += 1
        return pltpu.make_async_remote_copy(
            src_ref=src, dst_ref=dst, send_sem=send_sem.at[n], recv_sem=recv_sem.at[n],
            device_id=target, device_id_type=MESH,
        )

    unsent = []
    tick = [0]

    def send(src, dst, target):
        one = copy(src, dst, target)
        one.start()
        unsent.append((tick[0], one.wait_send))
        return one

    def drain(before):
        while unsent and unsent[0][0] < before:
            unsent.pop(0)[1]()

    def rows(ref, start, size):
        return ref.at[pl.ds(pl.multiple_of(start, 8), size)]

    def get(ref, start, size):
        return ref[pl.ds(pl.multiple_of(start, 8), size), :]

    def put(ref, start, size, value):
        ref[pl.ds(pl.multiple_of(start, 8), size), :] = value

    def basis_stage(s):
        width = WIDTHS[s]
        base = STARTS[s] * 4
        half = width * 2
        xr, zr = half // 4, half // 16
        za = zr // 2
        own = base + core * half
        mine = own + x * xr

        if s == 0:
            loads[0].wait()
            bt_in[...] = b_in[...].T
            loads[1].wait()
            value = dot(bt_in[...], tin[...], ((1,), (1,)))
        else:
            if s == 1:
                loads[4].wait()
            c = STARTS[s] - TOKENS
            value = dot(bt_in[...], qin[:, c:c + width])
        for tile in range(width // LANES):
            pb[base + tile * JB:base + (tile + 1) * JB, :] = value[:, tile * LANES:(tile + 1) * LANES]
        if s == 0:
            pl.semaphore_wait(barrier, len(peers))
        landing = ls.at[pl.ds(base // 2, half)]
        pair = send(rows(pb, base + (1 - core) * half, half), landing, sibling)
        yield

        pair.wait_recv()
        put(pb, own, half, get(pb, own, half) + ls[base // 2:base // 2 + half, :])
        lxo = base // 8
        sent = [
            send(rows(pb, own + ((x + d) % 4) * xr, xr), lx.at[d - 1, pl.ds(lxo, xr)], xs[d])
            for d in (2, 1, 3)
        ]
        yield

        for one in sent:
            one.wait_recv()
        put(pb, mine, xr, get(pb, mine, xr) + lx[0, lxo:lxo + xr, :]
            + lx[1, lxo:lxo + xr, :] + lx[2, lxo:lxo + xr, :])
        zo = base // 64

        def piece(p, second=0):
            return mine + ((zh + p) % 4) * zr + second * za

        def zland(ref, n):
            return ref.at[n, pl.ds(zo, za)]

        far_a = send(rows(pb, piece(2), za), zland(lz, 0), zhs[1])
        far_b = send(rows(pb, piece(2, 1), za), zland(lz, 2), zhs[3])
        near_b = send(rows(pb, piece(1, 1), za), zland(lz, 1), zhs[1])
        near_a = send(rows(pb, piece(3), za), zland(lz, 3), zhs[3])
        yield

        far_a.wait_recv()
        cz[0, zo:zo + za, :] = lz[0, zo:zo + za, :] + get(pb, piece(1), za)
        sum_a = send(zland(cz, 0), zland(lw, 0), zhs[1])
        far_b.wait_recv()
        cz[1, zo:zo + za, :] = lz[2, zo:zo + za, :] + get(pb, piece(3, 1), za)
        sum_b = send(zland(cz, 1), zland(lw, 1), zhs[3])
        yield

        near_a.wait_recv()
        near_b.wait_recv()
        sum_a.wait_recv()
        put(fb, piece(0), za, get(pb, piece(0), za) + lw[0, zo:zo + za, :] + lz[3, zo:zo + za, :])
        sum_b.wait_recv()
        put(fb, piece(0, 1), za, get(pb, piece(0, 1), za) + lw[1, zo:zo + za, :] + lz[1, zo:zo + za, :])
        up = send(rows(fb, piece(0), zr), rows(fb, piece(0), zr), zhs[1])
        down = send(rows(fb, piece(0), zr), rows(fb, piece(0), zr), zhs[3])
        yield

        up.wait_recv()
        up2 = send(rows(fb, piece(3), za), rows(fb, piece(3), za), zhs[1])
        down.wait_recv()
        down2 = send(rows(fb, piece(1, 1), za), rows(fb, piece(1, 1), za), zhs[3])
        yield

        up2.wait_recv()
        down2.wait_recv()
        sent = [send(rows(fb, mine, xr), rows(fb, mine, xr), xs[d]) for d in (2, 1, 3)]
        across = [send(rows(fb, mine, xr), rows(fb, mine, xr), sibling)]
        yield

        for d, one in zip((2, 1, 3), sent):
            one.wait_recv()
            place = own + ((x + 4 - d) % 4) * xr
            across.append(send(rows(fb, place, xr), rows(fb, place, xr), sibling))
        yield

        for one in across:
            one.wait_recv()

    def query_stage(s):
        width = WIDTHS[s]
        base = STARTS[s] * 2
        yr = width // 2
        mine = base + y * yr

        if s == 0:
            loads[2].wait()
            bt_out[...] = b_out[...].T
            loads[3].wait()
            value = dot(bt_out[...], tgr[...], ((1,), (1,)))
        else:
            if s == 1:
                loads[5].wait()
            c = STARTS[s] - TOKENS
            value = dot(bt_out[...], qout[:, c:c + width])
        for tile in range(width // LANES):
            pq[base + tile * IB:base + (tile + 1) * IB, :] = value[:, tile * LANES:(tile + 1) * LANES]
        lyo = base // 4
        sent = [
            send(rows(pq, base + ((y + d) % 4) * yr, yr), ly.at[d - 1, pl.ds(lyo, yr)], ys[d])
            for d in (2, 1, 3)
        ]
        yield

        for one in sent:
            one.wait_recv()
        put(pq, mine, yr, get(pq, mine, yr) + ly[0, lyo:lyo + yr, :]
            + ly[1, lyo:lyo + yr, :] + ly[2, lyo:lyo + yr, :])
        end = jnp.logical_or(zl == 0, zl == 3)
        middle = jnp.logical_or(zl == 1, zl == 2)
        inward = dev(zl=jnp.where(zl == 0, 1, 2))
        outward = dev(zl=jnp.where(zl == 1, 0, 3))
        over = dev(zl=3 - zl)
        block = rows(pq, mine, yr)
        done = rows(fq, mine, yr)
        to_middle = copy(block, le.at[pl.ds(lyo, yr)], inward)
        swap = copy(block, li.at[pl.ds(lyo, yr)], over)
        to_end = copy(done, done, outward)

        def when_sent(condition, one):
            def wait():
                @pl.when(condition)
                def _():
                    one.wait_send()

            unsent.append((tick[0], wait))

        @pl.when(end)
        def _():
            to_middle.start()

        when_sent(end, to_middle)
        yield

        @pl.when(middle)
        def _():
            to_middle.wait_recv()
            put(pq, mine, yr, get(pq, mine, yr) + le[lyo:lyo + yr, :])
            swap.start()

        when_sent(middle, swap)
        yield

        @pl.when(middle)
        def _():
            swap.wait_recv()
            put(fq, mine, yr, get(pq, mine, yr) + li[lyo:lyo + yr, :])
            to_end.start()

        when_sent(middle, to_end)
        yield

        @pl.when(end)
        def _():
            to_end.wait_recv()

        sent = [send(done, done, ys[d]) for d in (2, 1, 3)]
        yield

        for one in sent:
            one.wait_recv()

    def tiles(ref, base, count, size):
        return jnp.concatenate([ref[base + n * size:base + (n + 1) * size, :] for n in range(count)], axis=1)

    def make_scaled():
        g = tiles(fq, 0, 2, IB)
        a_hi, a_lo = split(tiles(fb, 0, 2, JB))
        g_hi, g_lo = split(g)
        loads[7].wait()
        zero = jnp.zeros_like(g_hi)
        total = None
        nt = ((1,), (1,))
        for n in range(EXAMPLES):
            mask = jnp.broadcast_to(eid[...] == n, (IB, TOKENS))
            high, low = jnp.where(mask, g_hi, zero), jnp.where(mask, g_lo, zero)
            scaled = (dot(high, a_hi, nt) + dot(high, a_lo, nt) + dot(low, a_hi, nt)) * inv[...]
            total = scaled if total is None else total + scaled
            hi, lo = split(scaled)
            s_hi[n] = hi
            s_lo[n] = lo
        o_total[...] = total.astype(jnp.bfloat16)

    def influence_of(s):
        width = WIDTHS[s]
        c = STARTS[s] - TOKENS
        count = width // LANES
        for first in range(0, count, 2):
            r_hi, r_lo = split(tiles(fb, STARTS[s] * 4 + first * JB, 2, JB))
            out = tiles(fq, STARTS[s] * 2 + first * IB, 2, IB)
            at = c + first * LANES
            for n in range(EXAMPLES):
                weighted = dot(s_hi[n], r_hi) + dot(s_hi[n], r_lo) + dot(s_lo[n], r_hi)
                part[n:n + 1, at:at + 2 * LANES] = jnp.sum(weighted * out, axis=0, keepdims=True)

    part[...] = jnp.zeros_like(part)
    running = []
    waiting = list(range(STAGES))
    while waiting or running:
        if waiting:
            s = waiting.pop(0)
            running.append([s, [basis_stage(s), query_stage(s)]])
        ended = []
        for item in running:
            alive = []
            for step in item[1]:
                try:
                    next(step)
                    alive.append(step)
                except StopIteration:
                    pass
            item[1] = alive
            if not alive:
                ended.append(item[0])
        running = [item for item in running if item[1]]
        if tick[0] == STAGES - 1:
            loads[6].wait()
            inv[...] = 1.0 / (eig[...] + DAMPING)
        for s in ended:
            if s == 0:
                make_scaled()
            else:
                influence_of(s)
        tick[0] += 1
        drain(tick[0] - 2)

    lane = lax.broadcasted_iota(jnp.int32, (QC, LANES), 1)
    row = lax.broadcasted_iota(jnp.int32, (QC, LANES), 0)
    value = select_dot(part[...], (row // RANK == lane).astype(jnp.bfloat16))

    def reduce(value, slots, index, targets):
        slots[index] = value
        sent = [send(slots.at[index], slots.at[index], target) for target in targets]
        for one in sent:
            one.wait_recv()
        total = slots[0]
        for n in range(1, slots.shape[0]):
            total = total + slots[n]
        return total

    value = reduce(value, ar_c, core, [sibling])
    value = reduce(value, ar_x, x, xs[1:])
    value = reduce(value, ar_y, y, ys[1:])
    value = reduce(value, ar_l, zl, zls[1:])
    value = reduce(value, ar_h, zh, zhs[1:])

    loads[8].wait()
    query_row = lax.broadcasted_iota(jnp.int32, (QUERIES, LANES), 1)
    table = (jnp.broadcast_to(tid[...], (QUERIES, LANES)) == query_row).astype(jnp.float32)
    counts = jnp.sum(table, axis=0, keepdims=True)
    padded = jnp.concatenate([table, jnp.zeros((LANES - QUERIES, LANES), jnp.float32)], axis=0)
    tasks = select_dot(value, padded.astype(jnp.bfloat16))
    o_inf[...] = value[:EXAMPLES, :QUERIES]
    o_task[...] = tasks[:EXAMPLES, :TASKS] / counts[:, :TASKS]
    drain(tick[0] + 1)


def shards(train_inputs, train_grads, example_ids, task_ids, basis_in, basis_out, eigenvalues, query_in, query_out):
    vm = pltpu.VMEM
    f32, bf16 = jnp.float32, jnp.bfloat16
    example_ids = example_ids.reshape(1, TOKENS)
    loaded = [
        vm(a.shape, a.dtype)
        for a in (train_inputs, train_grads, example_ids, task_ids, basis_in, basis_out, eigenvalues, query_in, query_out)
    ]
    scratch = loaded + [
        vm((JB, IB), bf16),
        vm((IB, JB), bf16),
        vm((IB, JB), f32),
        vm((TOTAL * 4, LANES), f32),
        vm((TOTAL * 4, LANES), f32),
        vm((TOTAL * 2, LANES), f32),
        vm((3, TOTAL // 2, LANES), f32),
        vm((4, TOTAL // 16, LANES), f32),
        vm((2, TOTAL // 16, LANES), f32),
        vm((2, TOTAL // 16, LANES), f32),
        vm((TOTAL * 2, LANES), f32),
        vm((TOTAL * 2, LANES), f32),
        vm((3, TOTAL // 2, LANES), f32),
        vm((TOTAL // 2, LANES), f32),
        vm((TOTAL // 2, LANES), f32),
        vm((EXAMPLES, IB, JB), bf16),
        vm((EXAMPLES, IB, JB), bf16),
        vm((8, QC), f32),
        vm((2, 8, LANES), f32),
        vm((4, 8, LANES), f32),
        vm((4, 8, LANES), f32),
        vm((4, 8, LANES), f32),
        vm((4, 8, LANES), f32),
        pltpu.SemaphoreType.DMA((COPIES,)),
        pltpu.SemaphoreType.DMA((COPIES,)),
        pltpu.SemaphoreType.DMA((9,)),
    ]
    return pl.pallas_call(
        kernel,
        out_shape=(
            jax.ShapeDtypeStruct((IB, JB), bf16),
            jax.ShapeDtypeStruct((EXAMPLES, QUERIES), f32),
            jax.ShapeDtypeStruct((EXAMPLES, TASKS), f32),
        ),
        in_specs=[pl.BlockSpec(memory_space=pl.ANY)] * 9,
        out_specs=[pl.BlockSpec(memory_space=pltpu.VMEM)] * 3,
        scratch_shapes=scratch,
        compiler_params=pltpu.CompilerParams(
            collective_id=0, has_side_effects=True, vmem_limit_bytes=52 * 2**20
        ),
        name="influence",
    )(train_inputs, train_grads, example_ids, task_ids, basis_in, basis_out, eigenvalues, query_in, query_out)


def solution(mesh):
    in_specs = (
        P(None, "basis"),
        P(None, "query"),
        P(),
        P(),
        P("basis", "query"),
        P("query", "basis"),
        P("basis", "query"),
        P("basis", None),
        P("query", None),
    )
    out_specs = (P("basis", "query"), P(), P())
    return jax.shard_map(shards, mesh=mesh, in_specs=in_specs, out_specs=out_specs, check_vma=False)
```

```python
import functools

import jax
import jax.numpy as jnp
from jax import lax
from jax.experimental import pallas as pl
from jax.experimental.pallas import tpu as pltpu
from jax.sharding import PartitionSpec as P

EXAMPLES = 4
QUERIES = 48
TASKS = 16
RANK = 32
DAMPING = 0.05
TOKENS = 256
QC = QUERIES * RANK
JB = 512
IB = 256
LANES = 128

WIDTHS = (256, 384, 384, 384, 384)
STARTS = tuple(sum(WIDTHS[:s]) for s in range(len(WIDTHS)))
STAGES = len(WIDTHS)
TOTAL = sum(WIDTHS)
ORDER = (
    (0, 0), (1, 1), (1, 4), (0, 0), (0, 2), (0, 2), (0, 4), (0, 0), (0, 4), (1, 0),
    (0, 1), (0, 3), (1, 1), (1, 4), (0, 2), (1, 2), (0, 1), (0, 0), (1, 0), (1, 1),
    (0, 4), (0, 3), (1, 4), (0, 2), (0, 0), (1, 3), (0, 1), (1, 4), (0, 4), (0, 3),
    (1, 0), (0, 2), (0, 1), (1, 4), (1, 0), (0, 4), (0, 0), (1, 2), (1, 3), (0, 3),
    (0, 2), (0, 1), (1, 0), (1, 4), (0, 0), (1, 1), (1, 2), (1, 3), (0, 4), (0, 3),
    (0, 2), (0, 1), (0, 0), (1, 1), (1, 2), (0, 4), (0, 3), (0, 1), (0, 0), (1, 3),
    (1, 2), (1, 0), (2, 0), (0, 3), (1, 3), (1, 1), (0, 4), (0, 1), (0, 2), (0, 4),
    (2, 4), (1, 2), (0, 1), (2, 1), (0, 3), (0, 2), (2, 2), (1, 3), (0, 3), (2, 3),
)
MESH = pl.DeviceIdType.MESH
COPIES = 200
EARLY = 1


def dot(a, b, contract=((1,), (0,))):
    return lax.dot_general(a, b, (contract, ((), ())), preferred_element_type=jnp.float32)


def split(value):
    high = value.astype(jnp.bfloat16)
    return high, (value - high.astype(jnp.float32)).astype(jnp.bfloat16)


def select_dot(value, table, contract=((1,), (0,))):
    high, rest = split(value)
    mid = (value - high.astype(jnp.float32) - rest.astype(jnp.float32)).astype(jnp.bfloat16)
    return dot(high, table, contract) + dot(rest, table, contract) + dot(mid, table, contract)


def kernel(
    h_tin, h_tgr, h_eid, h_tid, h_bin, h_bout, h_eig, h_qin, h_qout,
    o_total, o_inf, o_task,
    tin, tgr, eid, tid, b_in, b_out, eig, qin, qout,
    bt_in, bt_out, inv,
    pb, fb, ls, lx, lz, lw, cz, pq, fq, ly, le, li,
    s_hi, s_lo, part, ar_c, ar_p, ar_z,
    send_sem, recv_sem, load_sem,
):
    basis, query = lax.axis_index("basis"), lax.axis_index("query")
    zh, x, core = basis // 8, (basis // 2) % 4, basis % 2
    zl, y = query // 4, query % 4

    def dev(zh=zh, x=x, core=core, zl=zl, y=y):
        return (zh * 8 + x * 2 + core, zl * 4 + y)

    sibling = dev(core=1 - core)
    xs = [None] + [dev(x=(x + d) % 4) for d in (1, 2, 3)]
    ys = [None] + [dev(y=(y + d) % 4) for d in (1, 2, 3)]
    zhs = [None] + [dev(zh=(zh + d) % 4) for d in (1, 2, 3)]

    pairs = (
        (h_bin, b_in), (h_tin, tin), (h_bout, b_out), (h_tgr, tgr), (h_qin, qin),
        (h_qout, qout), (h_eig, eig), (h_eid, eid), (h_tid, tid),
    )
    loads = [pltpu.make_async_copy(src, dst, load_sem.at[n]) for n, (src, dst) in enumerate(pairs)]
    for load in loads[:4]:
        load.start()

    barrier = pltpu.get_barrier_semaphore()
    z = zh * 4 + zl
    plane = [dev(x=(x + a) % 4, y=(y + b) % 4) for a in (2, 1, 3, 0) for b in (2, 1, 3, 0) if a or b]
    far = sorted(range(1, 16), key=lambda d: abs(d - 8))
    column = [dev(zh=((z + d) % 16) // 4, zl=(z + d) % 4) for d in far]
    peers = column + plane + [sibling]
    for peer in peers:
        pl.semaphore_signal(barrier, inc=1, device_id=peer, device_id_type=MESH)
    for load in loads[4:]:
        load.start()

    made = [0]

    def copy(src, dst, target):
        n = made[0]
        made[0] += 1
        return pltpu.make_async_remote_copy(
            src_ref=src, dst_ref=dst, send_sem=send_sem.at[n], recv_sem=recv_sem.at[n],
            device_id=target, device_id_type=MESH,
        )

    unsent = []
    tick = [0]

    def send(src, dst, target):
        one = copy(src, dst, target)
        one.start()
        unsent.append((tick[0], one.wait_send))
        return one

    def drain(before):
        while unsent and unsent[0][0] < before:
            unsent.pop(0)[1]()

    def rows(ref, start, size):
        return ref.at[pl.ds(pl.multiple_of(start, 8), size)]

    def get(ref, start, size):
        return ref[pl.ds(pl.multiple_of(start, 8), size), :]

    def put(ref, start, size, value):
        ref[pl.ds(pl.multiple_of(start, 8), size), :] = value

    def basis_stage(s):
        width = WIDTHS[s]
        base = STARTS[s] * 4
        half = width * 2
        xr, zr = half // 4, half // 16
        za = zr // 2
        own = base + core * half
        mine = own + x * xr

        if s == 0:
            loads[0].wait()
            bt_in[...] = b_in[...].T
            loads[1].wait()
            value = dot(bt_in[...], tin[...], ((1,), (1,)))
        else:
            c = STARTS[s] - TOKENS
            value = dot(bt_in[...], qin[:, c:c + width])
        for tile in range(width // LANES):
            pb[base + tile * JB:base + (tile + 1) * JB, :] = value[:, tile * LANES:(tile + 1) * LANES]
        yield

        landing = ls.at[pl.ds(base // 2, half)]
        pair = send(rows(pb, base + (1 - core) * half, half), landing, sibling)
        yield

        pair.wait_recv()
        put(pb, own, half, get(pb, own, half) + ls[base // 2:base // 2 + half, :])
        lxo = base // 8
        sent = [
            send(rows(pb, own + ((x + d) % 4) * xr, xr), lx.at[d - 1, pl.ds(lxo, xr)], xs[d])
            for d in (2, 1, 3)
        ]
        yield

        for one in sent:
            one.wait_recv()
        put(pb, mine, xr, get(pb, mine, xr) + lx[0, lxo:lxo + xr, :]
            + lx[1, lxo:lxo + xr, :] + lx[2, lxo:lxo + xr, :])
        zo = base // 64

        def piece(p, second=0):
            return mine + ((zh + p) % 4) * zr + second * za

        def zland(ref, n):
            return ref.at[n, pl.ds(zo, za)]

        far_a = send(rows(pb, piece(2), za), zland(lz, 0), zhs[1])
        far_b = send(rows(pb, piece(2, 1), za), zland(lz, 2), zhs[3])
        near_b = send(rows(pb, piece(1, 1), za), zland(lz, 1), zhs[1])
        near_a = send(rows(pb, piece(3), za), zland(lz, 3), zhs[3])
        yield

        far_a.wait_recv()
        cz[0, zo:zo + za, :] = lz[0, zo:zo + za, :] + get(pb, piece(1), za)
        sum_a = send(zland(cz, 0), zland(lw, 0), zhs[1])
        far_b.wait_recv()
        cz[1, zo:zo + za, :] = lz[2, zo:zo + za, :] + get(pb, piece(3, 1), za)
        sum_b = send(zland(cz, 1), zland(lw, 1), zhs[3])
        yield

        near_a.wait_recv()
        near_b.wait_recv()
        sum_a.wait_recv()
        put(fb, piece(0), za, get(pb, piece(0), za) + lw[0, zo:zo + za, :] + lz[3, zo:zo + za, :])
        sum_b.wait_recv()
        put(fb, piece(0, 1), za, get(pb, piece(0, 1), za) + lw[1, zo:zo + za, :] + lz[1, zo:zo + za, :])
        up = send(rows(fb, piece(0), zr), rows(fb, piece(0), zr), zhs[1])
        down = send(rows(fb, piece(0), zr), rows(fb, piece(0), zr), zhs[3])
        yield

        up.wait_recv()
        up2 = send(rows(fb, piece(3), za), rows(fb, piece(3), za), zhs[1])
        down.wait_recv()
        down2 = send(rows(fb, piece(1, 1), za), rows(fb, piece(1, 1), za), zhs[3])
        yield

        up2.wait_recv()
        down2.wait_recv()
        sent = [send(rows(fb, mine, xr), rows(fb, mine, xr), xs[d]) for d in (2, 1, 3)]
        across = [send(rows(fb, mine, xr), rows(fb, mine, xr), sibling)]
        yield

        for d, one in zip((2, 1, 3), sent):
            one.wait_recv()
            place = own + ((x + 4 - d) % 4) * xr
            across.append(send(rows(fb, place, xr), rows(fb, place, xr), sibling))
        yield

        for one in across:
            one.wait_recv()

    def query_stage(s):
        width = WIDTHS[s]
        base = STARTS[s] * 2
        yr = width // 2
        mine = base + y * yr

        if s == 0:
            loads[2].wait()
            bt_out[...] = b_out[...].T
            loads[3].wait()
            value = dot(bt_out[...], tgr[...], ((1,), (1,)))
        else:
            c = STARTS[s] - TOKENS
            value = dot(bt_out[...], qout[:, c:c + width])
        for tile in range(width // LANES):
            pq[base + tile * IB:base + (tile + 1) * IB, :] = value[:, tile * LANES:(tile + 1) * LANES]
        yield

        lyo = base // 4
        sent = [
            send(rows(pq, base + ((y + d) % 4) * yr, yr), ly.at[d - 1, pl.ds(lyo, yr)], ys[d])
            for d in (2, 1, 3)
        ]
        yield

        for one in sent:
            one.wait_recv()
        put(pq, mine, yr, get(pq, mine, yr) + ly[0, lyo:lyo + yr, :]
            + ly[1, lyo:lyo + yr, :] + ly[2, lyo:lyo + yr, :])
        end = jnp.logical_or(zl == 0, zl == 3)
        middle = jnp.logical_or(zl == 1, zl == 2)
        inward = dev(zl=jnp.where(zl == 0, 1, 2))
        outward = dev(zl=jnp.where(zl == 1, 0, 3))
        over = dev(zl=3 - zl)
        block = rows(pq, mine, yr)
        done = rows(fq, mine, yr)
        to_middle = copy(block, le.at[pl.ds(lyo, yr)], inward)
        swap = copy(block, li.at[pl.ds(lyo, yr)], over)
        to_end = copy(done, done, outward)

        def when_sent(condition, one):
            def wait():
                @pl.when(condition)
                def _():
                    one.wait_send()

            unsent.append((tick[0], wait))

        @pl.when(end)
        def _():
            to_middle.start()

        when_sent(end, to_middle)
        yield

        @pl.when(middle)
        def _():
            to_middle.wait_recv()
            put(pq, mine, yr, get(pq, mine, yr) + le[lyo:lyo + yr, :])
            swap.start()

        when_sent(middle, swap)
        yield

        @pl.when(middle)
        def _():
            swap.wait_recv()
            put(fq, mine, yr, get(pq, mine, yr) + li[lyo:lyo + yr, :])
            to_end.start()

        when_sent(middle, to_end)
        yield

        @pl.when(end)
        def _():
            to_end.wait_recv()

        sent = [send(done, done, ys[d]) for d in (2, 1, 3)]
        yield

        for one in sent:
            one.wait_recv()

    def tiles(ref, base, count, size):
        return jnp.concatenate([ref[base + n * size:base + (n + 1) * size, :] for n in range(count)], axis=1)

    def make_scaled():
        g = tiles(fq, 0, 2, IB)
        a_hi, a_lo = split(tiles(fb, 0, 2, JB))
        g_hi, g_lo = split(g)
        loads[7].wait()
        zero = jnp.zeros_like(g_hi)
        total = None
        nt = ((1,), (1,))
        for n in range(EXAMPLES):
            mask = jnp.broadcast_to(eid[...] == n, (IB, TOKENS))
            high, low = jnp.where(mask, g_hi, zero), jnp.where(mask, g_lo, zero)
            scaled = (dot(high, a_hi, nt) + dot(high, a_lo, nt) + dot(low, a_hi, nt)) * inv[...]
            total = scaled if total is None else total + scaled
            hi, lo = split(scaled)
            s_hi[n] = hi
            s_lo[n] = lo
        o_total[...] = total.astype(jnp.bfloat16)

    def influence_of(s):
        width = WIDTHS[s]
        c = STARTS[s] - TOKENS
        count = width // LANES
        for first in range(0, count, 2):
            many = min(2, count - first)
            r_hi, r_lo = split(tiles(fb, STARTS[s] * 4 + first * JB, many, JB))
            out = tiles(fq, STARTS[s] * 2 + first * IB, many, IB)
            at = c + first * LANES
            for n in range(EXAMPLES):
                weighted = dot(s_hi[n], r_hi) + dot(s_hi[n], r_lo) + dot(s_lo[n], r_hi)
                part[n:n + 1, at:at + many * LANES] = jnp.sum(weighted * out, axis=0, keepdims=True)

    part[...] = jnp.zeros_like(part)
    begun = set()
    chains = [[basis_stage(s) for s in range(STAGES)], [query_stage(s) for s in range(STAGES)]]
    for s in range(EARLY):
        next(chains[0][s])
        next(chains[1][s])
    pl.semaphore_wait(barrier, len(peers))
    loads[4].wait()
    loads[5].wait()
    for kind, s in ORDER:
        if kind < 2 and s >= EARLY and (kind, s) not in begun:
            next(chains[kind][s])
            begun.add((kind, s))
        if kind < 2:
            next(chains[kind][s], None)
        elif s == 0:
            loads[6].wait()
            inv[...] = 1.0 / (eig[...] + DAMPING)
            make_scaled()
        else:
            influence_of(s)
        tick[0] += 1
        drain(tick[0] - 16)

    lane = lax.broadcasted_iota(jnp.int32, (QC, LANES), 1)
    row = lax.broadcasted_iota(jnp.int32, (QC, LANES), 0)
    value = select_dot(part[...], (row // RANK == lane).astype(jnp.bfloat16))

    def reduce(value, slots, index, targets):
        slots[index] = value
        sent = [send(slots.at[index], slots.at[index], target) for target in targets]
        for one in sent:
            one.wait_recv()
        total = slots[0]
        for n in range(1, slots.shape[0]):
            total = total + slots[n]
        return total

    value = reduce(value, ar_c, core, [sibling])
    value = reduce(value, ar_p, x * 4 + y, plane)
    value = reduce(value, ar_z, z, column)

    loads[8].wait()
    task = lax.broadcasted_iota(jnp.int32, (TASKS, QUERIES), 0)
    table = (jnp.broadcast_to(tid[...], (TASKS, QUERIES)) == task).astype(jnp.bfloat16)
    nt = ((1,), (1,))
    counts = dot(jnp.ones((8, QUERIES), jnp.bfloat16), table, nt)
    tasks = select_dot(value[:, :QUERIES], table, nt)
    o_inf[...] = value[:EXAMPLES, :QUERIES]
    o_task[...] = tasks[:EXAMPLES] / counts[:EXAMPLES]
    drain(tick[0] + 1)


def shards(train_inputs, train_grads, example_ids, task_ids, basis_in, basis_out, eigenvalues, query_in, query_out):
    vm = pltpu.VMEM
    f32, bf16 = jnp.float32, jnp.bfloat16
    example_ids = example_ids.reshape(1, TOKENS)
    task_ids = task_ids.reshape(1, QUERIES)
    loaded = [
        vm(a.shape, a.dtype)
        for a in (train_inputs, train_grads, example_ids, task_ids, basis_in, basis_out, eigenvalues, query_in, query_out)
    ]
    scratch = loaded + [
        vm((JB, IB), bf16),
        vm((IB, JB), bf16),
        vm((IB, JB), f32),
        vm((TOTAL * 4, LANES), f32),
        vm((TOTAL * 4, LANES), f32),
        vm((TOTAL * 2, LANES), f32),
        vm((3, TOTAL // 2, LANES), f32),
        vm((4, TOTAL // 16, LANES), f32),
        vm((2, TOTAL // 16, LANES), f32),
        vm((2, TOTAL // 16, LANES), f32),
        vm((TOTAL * 2, LANES), f32),
        vm((TOTAL * 2, LANES), f32),
        vm((3, TOTAL // 2, LANES), f32),
        vm((TOTAL // 2, LANES), f32),
        vm((TOTAL // 2, LANES), f32),
        vm((EXAMPLES, IB, JB), bf16),
        vm((EXAMPLES, IB, JB), bf16),
        vm((8, QC), f32),
        vm((2, 8, LANES), f32),
        vm((16, 8, LANES), f32),
        vm((16, 8, LANES), f32),
        pltpu.SemaphoreType.DMA((COPIES,)),
        pltpu.SemaphoreType.DMA((COPIES,)),
        pltpu.SemaphoreType.DMA((9,)),
    ]
    return pl.pallas_call(
        kernel,
        out_shape=(
            jax.ShapeDtypeStruct((IB, JB), bf16),
            jax.ShapeDtypeStruct((EXAMPLES, QUERIES), f32),
            jax.ShapeDtypeStruct((EXAMPLES, TASKS), f32),
        ),
        in_specs=[pl.BlockSpec(memory_space=pl.ANY)] * 9,
        out_specs=[pl.BlockSpec(memory_space=pltpu.VMEM)] * 3,
        scratch_shapes=scratch,
        compiler_params=pltpu.CompilerParams(
            collective_id=0, has_side_effects=True, vmem_limit_bytes=62 * 2**20
        ),
        name="influence",
    )(train_inputs, train_grads, example_ids, task_ids, basis_in, basis_out, eigenvalues, query_in, query_out)


def solution(mesh):
    in_specs = (
        P(None, "basis"),
        P(None, "query"),
        P(),
        P(),
        P("basis", "query"),
        P("query", "basis"),
        P("basis", "query"),
        P("basis", None),
        P("query", None),
    )
    out_specs = (P("basis", "query"), P(), P())
    return jax.shard_map(shards, mesh=mesh, in_specs=in_specs, out_specs=out_specs, check_vma=False)
```

```python
import functools

import jax
import jax.numpy as jnp
from jax import lax
from jax.experimental import pallas as pl
from jax.experimental.pallas import tpu as pltpu
from jax.sharding import PartitionSpec as P

EXAMPLES = 4
QUERIES = 48
TASKS = 16
RANK = 32
DAMPING = 0.05
TOKENS = 256
QC = QUERIES * RANK
JB = 512
IB = 256
LANES = 128

WIDTHS = (256, 256, 256, 256, 256, 256, 256)
STARTS = tuple(sum(WIDTHS[:s]) for s in range(len(WIDTHS)))
STAGES = len(WIDTHS)
TOTAL = sum(WIDTHS)
ORDER = (
    (0, 3), (1, 0), (0, 2), (1, 1), (0, 3), (0, 0), (0, 5), (0, 0), (1, 4), (1, 5),
    (0, 3), (0, 6), (0, 4), (0, 5), (1, 2), (0, 1), (1, 0), (1, 3), (0, 0), (0, 2),
    (1, 1), (0, 3), (0, 1), (1, 0), (0, 5), (0, 6), (1, 5), (1, 4), (0, 0), (0, 2),
    (0, 4), (1, 0), (0, 3), (1, 1), (0, 1), (0, 0), (0, 5), (0, 6), (1, 2), (1, 1),
    (0, 3), (0, 2), (1, 6), (0, 1), (0, 5), (1, 2), (0, 0), (0, 4), (1, 4), (0, 6),
    (1, 3), (0, 3), (0, 1), (1, 0), (1, 2), (1, 5), (0, 2), (1, 3), (0, 5), (0, 0),
    (0, 6), (1, 2), (1, 6), (0, 4), (0, 1), (1, 1), (1, 5), (1, 4), (0, 2), (0, 5),
    (1, 3), (0, 3), (1, 6), (0, 6), (0, 4), (0, 1), (1, 2), (1, 5), (1, 1), (0, 0),
    (1, 6), (0, 5), (1, 3), (0, 3), (0, 6), (0, 5), (0, 0), (0, 2), (0, 4), (1, 4),
    (0, 1), (1, 6), (1, 0), (2, 0), (0, 4), (1, 5), (2, 5), (0, 1), (2, 1), (0, 6),
    (0, 2), (1, 3), (2, 3), (0, 6), (1, 6), (2, 6), (0, 4), (0, 2), (2, 2), (1, 4),
    (0, 4), (2, 4),
)
MESH = pl.DeviceIdType.MESH
COPIES = 264
EARLY = 7


def dot(a, b, contract=((1,), (0,))):
    return lax.dot_general(a, b, (contract, ((), ())), preferred_element_type=jnp.float32)


def split(value):
    high = value.astype(jnp.bfloat16)
    return high, (value - high.astype(jnp.float32)).astype(jnp.bfloat16)


def select_dot(value, table, contract=((1,), (0,))):
    high, rest = split(value)
    mid = (value - high.astype(jnp.float32) - rest.astype(jnp.float32)).astype(jnp.bfloat16)
    return dot(high, table, contract) + dot(rest, table, contract) + dot(mid, table, contract)


def kernel(
    h_tin, h_tgr, h_eid, h_tid, h_bin, h_bout, h_eig, h_qin, h_qout,
    o_total, o_inf, o_task,
    tin, tgr, eid, tid, b_in, b_out, eig, qin, qout,
    bt_in, bt_out, inv, total_bf,
    pb, fb, ls, lx, lz, lw, cz, pq, fq, ly, le, li,
    s_hi, s_lo, part, ar_c, ar_p, ar_z,
    send_sem, recv_sem, load_sem,
):
    basis, query = lax.axis_index("basis"), lax.axis_index("query")
    zh, x, core = basis // 8, (basis // 2) % 4, basis % 2
    zl, y = query // 4, query % 4

    def dev(zh=zh, x=x, core=core, zl=zl, y=y):
        return (zh * 8 + x * 2 + core, zl * 4 + y)

    sibling = dev(core=1 - core)
    xs = [None] + [dev(x=(x + d) % 4) for d in (1, 2, 3)]
    ys = [None] + [dev(y=(y + d) % 4) for d in (1, 2, 3)]
    zhs = [None] + [dev(zh=(zh + d) % 4) for d in (1, 2, 3)]

    pairs = (
        (h_bin, b_in), (h_tin, tin), (h_bout, b_out), (h_tgr, tgr), (h_qin, qin),
        (h_qout, qout), (h_eig, eig), (h_eid, eid), (h_tid, tid),
    )
    loads = [pltpu.make_async_copy(src, dst, load_sem.at[n]) for n, (src, dst) in enumerate(pairs)]
    for load in loads[:4]:
        load.start()

    barrier = pltpu.get_barrier_semaphore()
    z = zh * 4 + zl
    plane = [dev(x=(x + a) % 4, y=(y + b) % 4) for a in (2, 1, 3, 0) for b in (2, 1, 3, 0) if a or b]
    far = sorted(range(1, 16), key=lambda d: abs(d - 8))
    column = [dev(zh=((z + d) % 16) // 4, zl=(z + d) % 4) for d in far]
    peers = column + plane + [sibling]
    for peer in peers:
        pl.semaphore_signal(barrier, inc=1, device_id=peer, device_id_type=MESH)
    for load in loads[4:]:
        load.start()

    made = [0]

    def copy(src, dst, target):
        n = made[0]
        made[0] += 1
        return pltpu.make_async_remote_copy(
            src_ref=src, dst_ref=dst, send_sem=send_sem.at[n], recv_sem=recv_sem.at[n],
            device_id=target, device_id_type=MESH,
        )

    unsent = []
    tick = [0]

    def send(src, dst, target):
        one = copy(src, dst, target)
        one.start()
        unsent.append((tick[0], one.wait_send))
        return one

    def drain(before):
        while unsent and unsent[0][0] < before:
            unsent.pop(0)[1]()

    def rows(ref, start, size):
        return ref.at[pl.ds(pl.multiple_of(start, 8), size)]

    def get(ref, start, size):
        return ref[pl.ds(pl.multiple_of(start, 8), size), :]

    def put(ref, start, size, value):
        ref[pl.ds(pl.multiple_of(start, 8), size), :] = value

    def basis_stage(s):
        width = WIDTHS[s]
        base = STARTS[s] * 4
        half = width * 2
        xr, zr = half // 4, half // 16
        za = zr // 2
        own = base + core * half
        mine = own + x * xr

        if s == 0:
            loads[0].wait()
            bt_in[...] = b_in[...].T
            loads[1].wait()
            value = dot(bt_in[...], tin[...], ((1,), (1,)))
        else:
            c = STARTS[s] - TOKENS
            value = dot(bt_in[...], qin[:, c:c + width])
        for tile in range(width // LANES):
            pb[base + tile * JB:base + (tile + 1) * JB, :] = value[:, tile * LANES:(tile + 1) * LANES]
        yield

        landing = ls.at[pl.ds(base // 2, half)]
        pair = send(rows(pb, base + (1 - core) * half, half), landing, sibling)
        yield

        pair.wait_recv()
        put(pb, own, half, get(pb, own, half) + ls[base // 2:base // 2 + half, :])
        lxo = base // 8
        sent = [
            send(rows(pb, own + ((x + d) % 4) * xr, xr), lx.at[d - 1, pl.ds(lxo, xr)], xs[d])
            for d in (2, 1, 3)
        ]
        yield

        for one in sent:
            one.wait_recv()
        put(pb, mine, xr, get(pb, mine, xr) + lx[0, lxo:lxo + xr, :]
            + lx[1, lxo:lxo + xr, :] + lx[2, lxo:lxo + xr, :])
        zo = base // 64

        def piece(p, second=0):
            return mine + ((zh + p) % 4) * zr + second * za

        def zland(ref, n):
            return ref.at[n, pl.ds(zo, za)]

        far_a = send(rows(pb, piece(2), za), zland(lz, 0), zhs[1])
        far_b = send(rows(pb, piece(2, 1), za), zland(lz, 2), zhs[3])
        near_b = send(rows(pb, piece(1, 1), za), zland(lz, 1), zhs[1])
        near_a = send(rows(pb, piece(3), za), zland(lz, 3), zhs[3])
        yield

        far_a.wait_recv()
        cz[0, zo:zo + za, :] = lz[0, zo:zo + za, :] + get(pb, piece(1), za)
        sum_a = send(zland(cz, 0), zland(lw, 0), zhs[1])
        far_b.wait_recv()
        cz[1, zo:zo + za, :] = lz[2, zo:zo + za, :] + get(pb, piece(3, 1), za)
        sum_b = send(zland(cz, 1), zland(lw, 1), zhs[3])
        yield

        near_a.wait_recv()
        near_b.wait_recv()
        sum_a.wait_recv()
        put(fb, piece(0), za, get(pb, piece(0), za) + lw[0, zo:zo + za, :] + lz[3, zo:zo + za, :])
        sum_b.wait_recv()
        put(fb, piece(0, 1), za, get(pb, piece(0, 1), za) + lw[1, zo:zo + za, :] + lz[1, zo:zo + za, :])
        up = send(rows(fb, piece(0), zr), rows(fb, piece(0), zr), zhs[1])
        down = send(rows(fb, piece(0), zr), rows(fb, piece(0), zr), zhs[3])
        yield

        up.wait_recv()
        up2 = send(rows(fb, piece(3), za), rows(fb, piece(3), za), zhs[1])
        down.wait_recv()
        down2 = send(rows(fb, piece(1, 1), za), rows(fb, piece(1, 1), za), zhs[3])
        yield

        up2.wait_recv()
        down2.wait_recv()
        sent = [send(rows(fb, mine, xr), rows(fb, mine, xr), xs[d]) for d in (2, 1, 3)]
        yield

        for one in sent:
            one.wait_recv()
        across = send(rows(fb, own, half), rows(fb, own, half), sibling)
        yield

        across.wait_recv()

    def query_stage(s):
        width = WIDTHS[s]
        base = STARTS[s] * 2
        yr = width // 2
        mine = base + y * yr

        if s == 0:
            loads[2].wait()
            bt_out[...] = b_out[...].T
            loads[3].wait()
            value = dot(bt_out[...], tgr[...], ((1,), (1,)))
        else:
            c = STARTS[s] - TOKENS
            value = dot(bt_out[...], qout[:, c:c + width])
        for tile in range(width // LANES):
            pq[base + tile * IB:base + (tile + 1) * IB, :] = value[:, tile * LANES:(tile + 1) * LANES]
        yield

        lyo = base // 4
        sent = [
            send(rows(pq, base + ((y + d) % 4) * yr, yr), ly.at[d - 1, pl.ds(lyo, yr)], ys[d])
            for d in (2, 1, 3)
        ]
        yield

        for one in sent:
            one.wait_recv()
        put(pq, mine, yr, get(pq, mine, yr) + ly[0, lyo:lyo + yr, :]
            + ly[1, lyo:lyo + yr, :] + ly[2, lyo:lyo + yr, :])
        end = jnp.logical_or(zl == 0, zl == 3)
        middle = jnp.logical_or(zl == 1, zl == 2)
        inward = dev(zl=jnp.where(zl == 0, 1, 2))
        outward = dev(zl=jnp.where(zl == 1, 0, 3))
        over = dev(zl=3 - zl)
        block = rows(pq, mine, yr)
        done = rows(fq, mine, yr)
        to_middle = copy(block, le.at[pl.ds(lyo, yr)], inward)
        swap = copy(block, li.at[pl.ds(lyo, yr)], over)
        to_end = copy(done, done, outward)

        def when_sent(condition, one):
            def wait():
                @pl.when(condition)
                def _():
                    one.wait_send()

            unsent.append((tick[0], wait))

        @pl.when(end)
        def _():
            to_middle.start()

        when_sent(end, to_middle)
        yield

        @pl.when(middle)
        def _():
            to_middle.wait_recv()
            put(pq, mine, yr, get(pq, mine, yr) + le[lyo:lyo + yr, :])
            swap.start()

        when_sent(middle, swap)
        yield

        @pl.when(middle)
        def _():
            swap.wait_recv()
            put(fq, mine, yr, get(pq, mine, yr) + li[lyo:lyo + yr, :])
            to_end.start()

        when_sent(middle, to_end)
        yield

        @pl.when(end)
        def _():
            to_end.wait_recv()

        sent = [send(done, done, ys[d]) for d in (2, 1, 3)]
        yield

        for one in sent:
            one.wait_recv()

    def tiles(ref, base, count, size):
        return jnp.concatenate([ref[base + n * size:base + (n + 1) * size, :] for n in range(count)], axis=1)

    store_total = pltpu.make_async_copy(total_bf, o_total, load_sem.at[9])

    def make_scaled():
        g = tiles(fq, 0, 2, IB)
        a_hi, a_lo = split(tiles(fb, 0, 2, JB))
        g_hi, g_lo = split(g)
        loads[7].wait()
        zero = jnp.zeros_like(g_hi)
        total = None
        nt = ((1,), (1,))
        for n in range(EXAMPLES):
            mask = jnp.broadcast_to(eid[...] == n, (IB, TOKENS))
            high, low = jnp.where(mask, g_hi, zero), jnp.where(mask, g_lo, zero)
            scaled = (dot(high, a_hi, nt) + dot(high, a_lo, nt) + dot(low, a_hi, nt)) * inv[...]
            total = scaled if total is None else total + scaled
            hi, lo = split(scaled)
            s_hi[n] = hi
            s_lo[n] = lo
        total_bf[...] = total.astype(jnp.bfloat16)
        store_total.start()

    def influence_of(s):
        width = WIDTHS[s]
        c = STARTS[s] - TOKENS
        count = width // LANES
        for first in range(0, count, 2):
            many = min(2, count - first)
            r_hi, r_lo = split(tiles(fb, STARTS[s] * 4 + first * JB, many, JB))
            out = tiles(fq, STARTS[s] * 2 + first * IB, many, IB)
            at = c + first * LANES
            for n in range(EXAMPLES):
                weighted = dot(s_hi[n], r_hi) + dot(s_hi[n], r_lo) + dot(s_lo[n], r_hi)
                part[n:n + 1, at:at + many * LANES] = jnp.sum(weighted * out, axis=0, keepdims=True)

    part[...] = jnp.zeros_like(part)
    begun = set()
    chains = [[basis_stage(s) for s in range(STAGES)], [query_stage(s) for s in range(STAGES)]]
    for s in range(EARLY):
        if s == 1:
            loads[4].wait()
            loads[5].wait()
        next(chains[0][s])
        next(chains[1][s])
    pl.semaphore_wait(barrier, len(peers))
    for kind, s in ORDER:
        if kind < 2 and s >= EARLY and (kind, s) not in begun:
            next(chains[kind][s])
            begun.add((kind, s))
        if kind < 2:
            next(chains[kind][s], None)
        elif s == 0:
            loads[6].wait()
            inv[...] = 1.0 / (eig[...] + DAMPING)
            make_scaled()
        else:
            influence_of(s)
        tick[0] += 1
        drain(tick[0] - 16)

    lane = lax.broadcasted_iota(jnp.int32, (QC, LANES), 1)
    row = lax.broadcasted_iota(jnp.int32, (QC, LANES), 0)
    value = select_dot(part[...], (row // RANK == lane).astype(jnp.bfloat16))

    def reduce(value, slots, index, targets):
        slots[index] = value
        sent = [send(slots.at[index], slots.at[index], target) for target in targets]
        for one in sent:
            one.wait_recv()
        total = slots[0]
        for n in range(1, slots.shape[0]):
            total = total + slots[n]
        return total

    value = reduce(value, ar_c, core, [sibling])
    value = reduce(value, ar_p, x * 4 + y, plane)
    value = reduce(value, ar_z, z, column)

    loads[8].wait()
    task = lax.broadcasted_iota(jnp.int32, (TASKS, QUERIES), 0)
    table = (jnp.broadcast_to(tid[...], (TASKS, QUERIES)) == task).astype(jnp.bfloat16)
    nt = ((1,), (1,))
    counts = dot(jnp.ones((8, QUERIES), jnp.bfloat16), table, nt)
    tasks = select_dot(value[:, :QUERIES], table, nt)
    o_inf[...] = value[:EXAMPLES, :QUERIES]
    o_task[...] = tasks[:EXAMPLES] / counts[:EXAMPLES]
    drain(tick[0] + 1)
    store_total.wait()


def finish(*refs):
    for src, dst in zip(refs[:3], refs[3:]):
        dst[...] = src[...]


def shards(train_inputs, train_grads, example_ids, task_ids, basis_in, basis_out, eigenvalues, query_in, query_out):
    vm = pltpu.VMEM
    f32, bf16 = jnp.float32, jnp.bfloat16
    example_ids = example_ids.reshape(1, TOKENS)
    task_ids = task_ids.reshape(1, QUERIES)
    loaded = [
        vm(a.shape, a.dtype)
        for a in (train_inputs, train_grads, example_ids, task_ids, basis_in, basis_out, eigenvalues, query_in, query_out)
    ]
    scratch = loaded + [
        vm((JB, IB), bf16),
        vm((IB, JB), bf16),
        vm((IB, JB), f32),
        vm((IB, JB), bf16),
        vm((TOTAL * 4, LANES), f32),
        vm((TOTAL * 4, LANES), f32),
        vm((TOTAL * 2, LANES), f32),
        vm((3, TOTAL // 2, LANES), f32),
        vm((4, TOTAL // 16, LANES), f32),
        vm((2, TOTAL // 16, LANES), f32),
        vm((2, TOTAL // 16, LANES), f32),
        vm((TOTAL * 2, LANES), f32),
        vm((TOTAL * 2, LANES), f32),
        vm((3, TOTAL // 2, LANES), f32),
        vm((TOTAL // 2, LANES), f32),
        vm((TOTAL // 2, LANES), f32),
        vm((EXAMPLES, IB, JB), bf16),
        vm((EXAMPLES, IB, JB), bf16),
        vm((8, QC), f32),
        vm((2, 8, LANES), f32),
        vm((16, 8, LANES), f32),
        vm((16, 8, LANES), f32),
        pltpu.SemaphoreType.DMA((COPIES,)),
        pltpu.SemaphoreType.DMA((COPIES,)),
        pltpu.SemaphoreType.DMA((10,)),
    ]
    shapes = (
        jax.ShapeDtypeStruct((IB, JB), bf16),
        jax.ShapeDtypeStruct((EXAMPLES, QUERIES), f32),
        jax.ShapeDtypeStruct((EXAMPLES, TASKS), f32),
    )
    results = pl.pallas_call(
        kernel,
        out_shape=shapes,
        in_specs=[pl.BlockSpec(memory_space=pl.ANY)] * 9,
        out_specs=[pl.BlockSpec(memory_space=pl.ANY)] + [pl.BlockSpec(memory_space=pltpu.VMEM)] * 2,
        scratch_shapes=scratch,
        compiler_params=pltpu.CompilerParams(
            collective_id=0, has_side_effects=True, vmem_limit_bytes=62 * 2**20
        ),
        name="influence",
    )(train_inputs, train_grads, example_ids, task_ids, basis_in, basis_out, eigenvalues, query_in, query_out)
    return pl.pallas_call(
        finish,
        out_shape=shapes,
        in_specs=[pl.BlockSpec(memory_space=pltpu.VMEM)] * 3,
        out_specs=[pl.BlockSpec(memory_space=pltpu.VMEM)] * 3,
        compiler_params=pltpu.CompilerParams(vmem_limit_bytes=62 * 2**20),
        name="finish",
    )(*results)


def solution(mesh):
    in_specs = (
        P(None, "basis"),
        P(None, "query"),
        P(),
        P(),
        P("basis", "query"),
        P("query", "basis"),
        P("basis", "query"),
        P("basis", None),
        P("query", None),
    )
    out_specs = (P("basis", "query"), P(), P())
    return jax.shard_map(shards, mesh=mesh, in_specs=in_specs, out_specs=out_specs, check_vma=False)
```

```python
import functools

import jax
import jax.numpy as jnp
from jax import lax
from jax.experimental import pallas as pl
from jax.experimental.pallas import tpu as pltpu
from jax.sharding import PartitionSpec as P

EXAMPLES = 4
QUERIES = 48
TASKS = 16
RANK = 32
DAMPING = 0.05
TOKENS = 256
QC = QUERIES * RANK
JB = 512
IB = 256
LANES = 128

WIDTHS = (256, 256, 256, 256, 256, 256, 256)
STARTS = tuple(sum(WIDTHS[:s]) for s in range(len(WIDTHS)))
STAGES = len(WIDTHS)
TOTAL = sum(WIDTHS)
ORDER = (
    (1, 5), (0, 4), (0, 4), (0, 0), (1, 0), (0, 1), (0, 0), (0, 5), (0, 5), (0, 3),
    (1, 4), (1, 0), (0, 4), (1, 3), (0, 6), (0, 1), (0, 2), (1, 5), (0, 0), (1, 0),
    (0, 3), (0, 5), (1, 5), (0, 4), (1, 3), (0, 1), (0, 2), (0, 6), (1, 4), (0, 0),
    (0, 3), (1, 3), (1, 0), (0, 4), (1, 1), (0, 1), (1, 2), (1, 5), (0, 0), (0, 3),
    (0, 2), (1, 6), (0, 5), (0, 6), (0, 4), (1, 4), (0, 3), (0, 1), (1, 3), (0, 2),
    (1, 6), (1, 0), (1, 1), (0, 4), (0, 0), (1, 5), (1, 2), (0, 5), (0, 6), (0, 3),
    (1, 4), (1, 1), (0, 2), (1, 3), (0, 0), (1, 2), (0, 1), (1, 0), (0, 6), (0, 4),
    (1, 4), (0, 5), (0, 3), (1, 6), (1, 1), (1, 2), (0, 2), (1, 5), (1, 3), (0, 1),
    (0, 4), (0, 5), (0, 6), (0, 0), (1, 2), (1, 6), (1, 1), (0, 3), (0, 2), (0, 0),
    (2, 0), (0, 6), (1, 6), (0, 1), (1, 4), (2, 4), (0, 5), (0, 3), (2, 3), (0, 2),
    (1, 2), (1, 1), (0, 1), (2, 1), (0, 5), (2, 5), (0, 6), (1, 6), (0, 2), (2, 2),
    (0, 6), (2, 6),
)
MESH = pl.DeviceIdType.MESH
COPIES = 264
EARLY = 7


def dot(a, b, contract=((1,), (0,))):
    return lax.dot_general(a, b, (contract, ((), ())), preferred_element_type=jnp.float32)


def split(value):
    high = value.astype(jnp.bfloat16)
    return high, (value - high.astype(jnp.float32)).astype(jnp.bfloat16)


def select_dot(value, table, contract=((1,), (0,))):
    high, rest = split(value)
    mid = (value - high.astype(jnp.float32) - rest.astype(jnp.float32)).astype(jnp.bfloat16)
    return dot(high, table, contract) + dot(rest, table, contract) + dot(mid, table, contract)


def kernel(
    h_tin, h_tgr, h_eid, h_tid, h_bin, h_bout, h_eig, h_qin, h_qout,
    o_total, o_inf, o_task,
    tin, tgr, eid, tid, b_in, b_out, eig, qin, qout,
    bt_in, bt_out, inv, total_bf, chosen,
    pb, fb, ls, lx, lz, lw, cz, pq, fq, ly, le, li,
    s_hi, s_lo, part, ar_c, ar_p, ar_z,
    send_sem, recv_sem, load_sem,
):
    basis, query = lax.axis_index("basis"), lax.axis_index("query")
    zh, x, core = basis // 8, (basis // 2) % 4, basis % 2
    zl, y = query // 4, query % 4

    def dev(zh=zh, x=x, core=core, zl=zl, y=y):
        return (zh * 8 + x * 2 + core, zl * 4 + y)

    sibling = dev(core=1 - core)
    xs = [None] + [dev(x=(x + d) % 4) for d in (1, 2, 3)]
    ys = [None] + [dev(y=(y + d) % 4) for d in (1, 2, 3)]
    zhs = [None] + [dev(zh=(zh + d) % 4) for d in (1, 2, 3)]

    pairs = (
        (h_bin, b_in), (h_tin, tin), (h_bout, b_out), (h_tgr, tgr), (h_qin, qin),
        (h_qout, qout), (h_eig, eig), (h_eid, eid), (h_tid, tid),
    )
    loads = [pltpu.make_async_copy(src, dst, load_sem.at[n]) for n, (src, dst) in enumerate(pairs)]
    for load in loads[:4]:
        load.start()

    barrier = pltpu.get_barrier_semaphore()
    z = zh * 4 + zl
    plane = [dev(x=(x + a) % 4, y=(y + b) % 4) for a in (2, 1, 3, 0) for b in (2, 1, 3, 0) if a or b]
    far = sorted(range(1, 16), key=lambda d: abs(d - 8))
    column = [dev(zh=((z + d) % 16) // 4, zl=(z + d) % 4) for d in far]
    peers = column + plane + [sibling]
    for peer in peers:
        pl.semaphore_signal(barrier, inc=1, device_id=peer, device_id_type=MESH)
    for load in loads[4:]:
        load.start()

    made = [0]

    def copy(src, dst, target):
        n = made[0]
        made[0] += 1
        return pltpu.make_async_remote_copy(
            src_ref=src, dst_ref=dst, send_sem=send_sem.at[n], recv_sem=recv_sem.at[n],
            device_id=target, device_id_type=MESH,
        )

    unsent = []
    tick = [0]

    def send(src, dst, target):
        one = copy(src, dst, target)
        one.start()
        unsent.append((tick[0], one.wait_send))
        return one

    def drain(before):
        while unsent and unsent[0][0] < before:
            unsent.pop(0)[1]()

    def rows(ref, start, size):
        return ref.at[pl.ds(pl.multiple_of(start, 8), size)]

    def get(ref, start, size):
        return ref[pl.ds(pl.multiple_of(start, 8), size), :]

    def put(ref, start, size, value):
        ref[pl.ds(pl.multiple_of(start, 8), size), :] = value

    def basis_stage(s):
        width = WIDTHS[s]
        base = STARTS[s] * 4
        half = width * 2
        xr, zr = half // 4, half // 16
        za = zr // 2
        own = base + core * half
        mine = own + x * xr

        if s == 0:
            loads[0].wait()
            bt_in[...] = b_in[...].T
            loads[1].wait()
            value = dot(bt_in[...], tin[...], ((1,), (1,)))
        else:
            c = STARTS[s] - TOKENS
            value = dot(bt_in[...], qin[:, c:c + width])
        for tile in range(width // LANES):
            pb[base + tile * JB:base + (tile + 1) * JB, :] = value[:, tile * LANES:(tile + 1) * LANES]
        yield

        landing = ls.at[pl.ds(base // 2, half)]
        pair = send(rows(pb, base + (1 - core) * half, half), landing, sibling)
        yield

        pair.wait_recv()
        put(pb, own, half, get(pb, own, half) + ls[base // 2:base // 2 + half, :])
        lxo = base // 8
        sent = [
            send(rows(pb, own + ((x + d) % 4) * xr, xr), lx.at[d - 1, pl.ds(lxo, xr)], xs[d])
            for d in (2, 1, 3)
        ]
        yield

        for one in sent:
            one.wait_recv()
        put(pb, mine, xr, get(pb, mine, xr) + lx[0, lxo:lxo + xr, :]
            + lx[1, lxo:lxo + xr, :] + lx[2, lxo:lxo + xr, :])
        zo = base // 64

        def piece(p, second=0):
            return mine + ((zh + p) % 4) * zr + second * za

        def zland(ref, n):
            return ref.at[n, pl.ds(zo, za)]

        far_a = send(rows(pb, piece(2), za), zland(lz, 0), zhs[1])
        far_b = send(rows(pb, piece(2, 1), za), zland(lz, 2), zhs[3])
        near_b = send(rows(pb, piece(1, 1), za), zland(lz, 1), zhs[1])
        near_a = send(rows(pb, piece(3), za), zland(lz, 3), zhs[3])
        yield

        far_a.wait_recv()
        cz[0, zo:zo + za, :] = lz[0, zo:zo + za, :] + get(pb, piece(1), za)
        sum_a = send(zland(cz, 0), zland(lw, 0), zhs[1])
        far_b.wait_recv()
        cz[1, zo:zo + za, :] = lz[2, zo:zo + za, :] + get(pb, piece(3, 1), za)
        sum_b = send(zland(cz, 1), zland(lw, 1), zhs[3])
        yield

        near_a.wait_recv()
        near_b.wait_recv()
        sum_a.wait_recv()
        put(fb, piece(0), za, get(pb, piece(0), za) + lw[0, zo:zo + za, :] + lz[3, zo:zo + za, :])
        sum_b.wait_recv()
        put(fb, piece(0, 1), za, get(pb, piece(0, 1), za) + lw[1, zo:zo + za, :] + lz[1, zo:zo + za, :])
        up = send(rows(fb, piece(0), zr), rows(fb, piece(0), zr), zhs[1])
        down = send(rows(fb, piece(0), zr), rows(fb, piece(0), zr), zhs[3])
        yield

        up.wait_recv()
        up2 = send(rows(fb, piece(3), za), rows(fb, piece(3), za), zhs[1])
        down.wait_recv()
        down2 = send(rows(fb, piece(1, 1), za), rows(fb, piece(1, 1), za), zhs[3])
        yield

        up2.wait_recv()
        down2.wait_recv()
        sent = [send(rows(fb, mine, xr), rows(fb, mine, xr), xs[d]) for d in (2, 1, 3)]
        yield

        for one in sent:
            one.wait_recv()
        across = send(rows(fb, own, half), rows(fb, own, half), sibling)
        yield

        across.wait_recv()

    def query_stage(s):
        width = WIDTHS[s]
        base = STARTS[s] * 2
        yr = width // 2
        mine = base + y * yr

        if s == 0:
            loads[2].wait()
            bt_out[...] = b_out[...].T
            loads[3].wait()
            value = dot(bt_out[...], tgr[...], ((1,), (1,)))
        else:
            c = STARTS[s] - TOKENS
            value = dot(bt_out[...], qout[:, c:c + width])
        for tile in range(width // LANES):
            pq[base + tile * IB:base + (tile + 1) * IB, :] = value[:, tile * LANES:(tile + 1) * LANES]
        yield

        lyo = base // 4
        sent = [
            send(rows(pq, base + ((y + d) % 4) * yr, yr), ly.at[d - 1, pl.ds(lyo, yr)], ys[d])
            for d in (2, 1, 3)
        ]
        yield

        for one in sent:
            one.wait_recv()
        put(pq, mine, yr, get(pq, mine, yr) + ly[0, lyo:lyo + yr, :]
            + ly[1, lyo:lyo + yr, :] + ly[2, lyo:lyo + yr, :])
        end = jnp.logical_or(zl == 0, zl == 3)
        middle = jnp.logical_or(zl == 1, zl == 2)
        inward = dev(zl=jnp.where(zl == 0, 1, 2))
        outward = dev(zl=jnp.where(zl == 1, 0, 3))
        over = dev(zl=3 - zl)
        block = rows(pq, mine, yr)
        done = rows(fq, mine, yr)
        to_middle = copy(block, le.at[pl.ds(lyo, yr)], inward)
        swap = copy(block, li.at[pl.ds(lyo, yr)], over)
        to_end = copy(done, done, outward)

        def when_sent(condition, one):
            def wait():
                @pl.when(condition)
                def _():
                    one.wait_send()

            unsent.append((tick[0], wait))

        @pl.when(end)
        def _():
            to_middle.start()

        when_sent(end, to_middle)
        yield

        @pl.when(middle)
        def _():
            to_middle.wait_recv()
            put(pq, mine, yr, get(pq, mine, yr) + le[lyo:lyo + yr, :])
            swap.start()

        when_sent(middle, swap)
        yield

        @pl.when(middle)
        def _():
            swap.wait_recv()
            put(fq, mine, yr, get(pq, mine, yr) + li[lyo:lyo + yr, :])
            to_end.start()

        when_sent(middle, to_end)
        yield

        @pl.when(end)
        def _():
            to_end.wait_recv()

        sent = [send(done, done, ys[d]) for d in (2, 1, 3)]
        yield

        for one in sent:
            one.wait_recv()

    def tiles(ref, base, count, size):
        return jnp.concatenate([ref[base + n * size:base + (n + 1) * size, :] for n in range(count)], axis=1)

    store_total = pltpu.make_async_copy(total_bf, o_total, load_sem.at[9])

    def make_scaled():
        g = tiles(fq, 0, 2, IB)
        a_hi, a_lo = split(tiles(fb, 0, 2, JB))
        g_hi, g_lo = split(g)
        loads[7].wait()
        zero = jnp.zeros_like(g_hi)
        total = None
        nt = ((1,), (1,))
        for n in range(EXAMPLES):
            mask = jnp.broadcast_to(eid[...] == n, (IB, TOKENS))
            high, low = jnp.where(mask, g_hi, zero), jnp.where(mask, g_lo, zero)
            scaled = (dot(high, a_hi, nt) + dot(high, a_lo, nt) + dot(low, a_hi, nt)) * inv[...]
            total = scaled if total is None else total + scaled
            hi, lo = split(scaled)
            s_hi[n] = hi
            s_lo[n] = lo
        total_bf[...] = total.astype(jnp.bfloat16)
        store_total.start()

    def influence_of(s):
        width = WIDTHS[s]
        c = STARTS[s] - TOKENS
        count = width // LANES
        for first in range(0, count, 2):
            many = min(2, count - first)
            r_hi, r_lo = split(tiles(fb, STARTS[s] * 4 + first * JB, many, JB))
            out = tiles(fq, STARTS[s] * 2 + first * IB, many, IB)
            at = c + first * LANES
            for n in range(EXAMPLES):
                weighted = dot(s_hi[n], r_hi) + dot(s_hi[n], r_lo) + dot(s_lo[n], r_hi)
                part[n:n + 1, at:at + many * LANES] = jnp.sum(weighted * out, axis=0, keepdims=True)

    part[...] = jnp.zeros_like(part)
    begun = set()
    chains = [[basis_stage(s) for s in range(STAGES)], [query_stage(s) for s in range(STAGES)]]
    for s in range(EARLY):
        if s == 1:
            loads[4].wait()
            loads[5].wait()
        next(chains[0][s])
        next(chains[1][s])
    pl.semaphore_wait(barrier, len(peers))
    for kind, s in ORDER:
        if kind < 2 and s >= EARLY and (kind, s) not in begun:
            next(chains[kind][s])
            begun.add((kind, s))
        if kind < 2:
            next(chains[kind][s], None)
        elif s == 0:
            loads[6].wait()
            inv[...] = 1.0 / (eig[...] + DAMPING)
            make_scaled()
            lane = lax.broadcasted_iota(jnp.int32, (QC, LANES), 1)
            row = lax.broadcasted_iota(jnp.int32, (QC, LANES), 0)
            chosen[...] = (row // RANK == lane).astype(jnp.bfloat16)
        else:
            influence_of(s)
        tick[0] += 1
        drain(tick[0] - 16)

    value = select_dot(part[...], chosen[...])

    def reduce(value, slots, index, targets):
        slots[index] = value
        sent = [send(slots.at[index], slots.at[index], target) for target in targets]
        for one in sent:
            one.wait_recv()
        total = slots[0]
        for n in range(1, slots.shape[0]):
            total = total + slots[n]
        return total

    value = reduce(value, ar_c, core, [sibling])
    value = reduce(value, ar_p, x * 4 + y, plane)
    value = reduce(value, ar_z, z, column)

    loads[8].wait()
    task = lax.broadcasted_iota(jnp.int32, (TASKS, QUERIES), 0)
    table = (jnp.broadcast_to(tid[...], (TASKS, QUERIES)) == task).astype(jnp.bfloat16)
    nt = ((1,), (1,))
    counts = dot(jnp.ones((8, QUERIES), jnp.bfloat16), table, nt)
    tasks = select_dot(value[:, :QUERIES], table, nt)
    o_inf[...] = value[:EXAMPLES, :QUERIES]
    o_task[...] = tasks[:EXAMPLES] / counts[:EXAMPLES]
    drain(tick[0] + 1)
    store_total.wait()


def finish(*refs):
    for src, dst in zip(refs[:3], refs[3:]):
        dst[...] = src[...]


def shards(train_inputs, train_grads, example_ids, task_ids, basis_in, basis_out, eigenvalues, query_in, query_out):
    vm = pltpu.VMEM
    f32, bf16 = jnp.float32, jnp.bfloat16
    example_ids = example_ids.reshape(1, TOKENS)
    task_ids = task_ids.reshape(1, QUERIES)
    loaded = [
        vm(a.shape, a.dtype)
        for a in (train_inputs, train_grads, example_ids, task_ids, basis_in, basis_out, eigenvalues, query_in, query_out)
    ]
    scratch = loaded + [
        vm((JB, IB), bf16),
        vm((IB, JB), bf16),
        vm((IB, JB), f32),
        vm((IB, JB), bf16),
        vm((QC, LANES), bf16),
        vm((TOTAL * 4, LANES), f32),
        vm((TOTAL * 4, LANES), f32),
        vm((TOTAL * 2, LANES), f32),
        vm((3, TOTAL // 2, LANES), f32),
        vm((4, TOTAL // 16, LANES), f32),
        vm((2, TOTAL // 16, LANES), f32),
        vm((2, TOTAL // 16, LANES), f32),
        vm((TOTAL * 2, LANES), f32),
        vm((TOTAL * 2, LANES), f32),
        vm((3, TOTAL // 2, LANES), f32),
        vm((TOTAL // 2, LANES), f32),
        vm((TOTAL // 2, LANES), f32),
        vm((EXAMPLES, IB, JB), bf16),
        vm((EXAMPLES, IB, JB), bf16),
        vm((8, QC), f32),
        vm((2, 8, LANES), f32),
        vm((16, 8, LANES), f32),
        vm((16, 8, LANES), f32),
        pltpu.SemaphoreType.DMA((COPIES,)),
        pltpu.SemaphoreType.DMA((COPIES,)),
        pltpu.SemaphoreType.DMA((10,)),
    ]
    shapes = (
        jax.ShapeDtypeStruct((IB, JB), bf16),
        jax.ShapeDtypeStruct((EXAMPLES, QUERIES), f32),
        jax.ShapeDtypeStruct((EXAMPLES, TASKS), f32),
    )
    results = pl.pallas_call(
        kernel,
        out_shape=shapes,
        in_specs=[pl.BlockSpec(memory_space=pl.ANY)] * 9,
        out_specs=[pl.BlockSpec(memory_space=pl.ANY)] + [pl.BlockSpec(memory_space=pltpu.VMEM)] * 2,
        scratch_shapes=scratch,
        compiler_params=pltpu.CompilerParams(
            collective_id=0, has_side_effects=True, vmem_limit_bytes=62 * 2**20
        ),
        name="influence",
    )(train_inputs, train_grads, example_ids, task_ids, basis_in, basis_out, eigenvalues, query_in, query_out)
    return pl.pallas_call(
        finish,
        out_shape=shapes,
        in_specs=[pl.BlockSpec(memory_space=pltpu.VMEM)] * 3,
        out_specs=[pl.BlockSpec(memory_space=pltpu.VMEM)] * 3,
        compiler_params=pltpu.CompilerParams(vmem_limit_bytes=62 * 2**20),
        name="finish",
    )(*results)


def solution(mesh):
    in_specs = (
        P(None, "basis"),
        P(None, "query"),
        P(),
        P(),
        P("basis", "query"),
        P("query", "basis"),
        P("basis", "query"),
        P("basis", None),
        P("query", None),
    )
    out_specs = (P("basis", "query"), P(), P())
    return jax.shard_map(shards, mesh=mesh, in_specs=in_specs, out_specs=out_specs, check_vma=False)
```

```python
import functools

import jax
import jax.numpy as jnp
from jax import lax
from jax.experimental import pallas as pl
from jax.experimental.pallas import tpu as pltpu
from jax.sharding import PartitionSpec as P

EXAMPLES = 4
QUERIES = 48
TASKS = 16
RANK = 32
DAMPING = 0.05
TOKENS = 256
QC = QUERIES * RANK
JB = 512
IB = 256
LANES = 128

WIDTHS = (256, 256, 256, 256, 256, 256, 256)
STARTS = tuple(sum(WIDTHS[:s]) for s in range(len(WIDTHS)))
STAGES = len(WIDTHS)
TOTAL = sum(WIDTHS)
ORDER = (
    (1, 5), (0, 4), (0, 4), (0, 0), (1, 0), (0, 1), (0, 0), (0, 5), (0, 5), (0, 3),
    (1, 4), (1, 0), (0, 4), (1, 3), (0, 6), (0, 1), (0, 2), (1, 5), (0, 0), (1, 0),
    (0, 3), (0, 5), (1, 5), (0, 4), (1, 3), (0, 1), (0, 2), (0, 6), (1, 4), (0, 0),
    (0, 3), (1, 3), (1, 0), (0, 4), (1, 1), (0, 1), (1, 2), (1, 5), (0, 0), (0, 3),
    (0, 2), (1, 6), (0, 5), (0, 6), (0, 4), (1, 4), (0, 3), (0, 1), (1, 3), (0, 2),
    (1, 6), (1, 0), (1, 1), (0, 4), (0, 0), (1, 5), (1, 2), (0, 5), (0, 6), (0, 3),
    (1, 4), (1, 1), (0, 2), (1, 3), (0, 0), (1, 2), (0, 1), (1, 0), (0, 6), (0, 4),
    (1, 4), (0, 5), (0, 3), (1, 6), (1, 1), (1, 2), (0, 2), (1, 5), (1, 3), (0, 1),
    (0, 4), (0, 5), (0, 6), (0, 0), (1, 2), (1, 6), (1, 1), (0, 3), (0, 2), (0, 0),
    (2, 0), (0, 6), (1, 6), (0, 1), (1, 4), (2, 4), (0, 5), (0, 3), (2, 3), (0, 2),
    (1, 2), (1, 1), (0, 1), (2, 1), (0, 5), (2, 5), (0, 6), (1, 6), (0, 2), (2, 2),
    (0, 6), (2, 6),
)
MESH = pl.DeviceIdType.MESH
COPIES = 264


def dot(a, b, contract=((1,), (0,))):
    return lax.dot_general(a, b, (contract, ((), ())), preferred_element_type=jnp.float32)


def split(value):
    high = value.astype(jnp.bfloat16)
    return high, (value - high.astype(jnp.float32)).astype(jnp.bfloat16)


def select_dot(value, table, contract=((1,), (0,))):
    high, rest = split(value)
    mid = (value - high.astype(jnp.float32) - rest.astype(jnp.float32)).astype(jnp.bfloat16)
    return dot(high, table, contract) + dot(rest, table, contract) + dot(mid, table, contract)


def kernel(
    h_tin, h_tgr, h_eid, h_tid, h_bin, h_bout, h_eig, h_qin, h_qout,
    o_total, o_inf, o_task,
    tin, tgr, eid, tid, b_in, b_out, eig, qin, qout,
    bt_in, bt_out, inv, total_bf, chosen,
    pb, fb, ls, lx, lz, lw, cz, pq, fq, ly, le, li,
    s_hi, s_lo, part, ar_c, ar_p, ar_z,
    send_sem, recv_sem, load_sem,
):
    basis, query = lax.axis_index("basis"), lax.axis_index("query")
    zh, x, core = basis // 8, (basis // 2) % 4, basis % 2
    zl, y = query // 4, query % 4

    def dev(zh=zh, x=x, core=core, zl=zl, y=y):
        return (zh * 8 + x * 2 + core, zl * 4 + y)

    sibling = dev(core=1 - core)
    xs = [None] + [dev(x=(x + d) % 4) for d in (1, 2, 3)]
    ys = [None] + [dev(y=(y + d) % 4) for d in (1, 2, 3)]
    zhs = [None] + [dev(zh=(zh + d) % 4) for d in (1, 2, 3)]

    pairs = (
        (h_bin, b_in), (h_tin, tin), (h_bout, b_out), (h_tgr, tgr), (h_qin, qin),
        (h_qout, qout), (h_eig, eig), (h_eid, eid), (h_tid, tid),
    )
    loads = [pltpu.make_async_copy(src, dst, load_sem.at[n]) for n, (src, dst) in enumerate(pairs)]
    for load in loads[:4]:
        load.start()

    barrier = pltpu.get_barrier_semaphore()
    z = zh * 4 + zl
    plane = [dev(x=(x + a) % 4, y=(y + b) % 4) for a in (2, 1, 3, 0) for b in (2, 1, 3, 0) if a or b]
    far = sorted(range(1, 16), key=lambda d: abs(d - 8))
    column = [dev(zh=((z + d) % 16) // 4, zl=(z + d) % 4) for d in far]
    peers = column + plane + [sibling]
    for peer in peers:
        pl.semaphore_signal(barrier, inc=1, device_id=peer, device_id_type=MESH)
    for load in loads[4:]:
        load.start()

    made = [0]

    def copy(src, dst, target):
        n = made[0]
        made[0] += 1
        return pltpu.make_async_remote_copy(
            src_ref=src, dst_ref=dst, send_sem=send_sem.at[n], recv_sem=recv_sem.at[n],
            device_id=target, device_id_type=MESH,
        )

    unsent = []
    tick = [0]

    def send(src, dst, target):
        one = copy(src, dst, target)
        one.start()
        unsent.append((tick[0], one.wait_send))
        return one

    def drain(before):
        while unsent and unsent[0][0] < before:
            unsent.pop(0)[1]()

    def rows(ref, start, size):
        return ref.at[pl.ds(pl.multiple_of(start, 8), size)]

    def get(ref, start, size):
        return ref[pl.ds(pl.multiple_of(start, 8), size), :]

    def put(ref, start, size, value):
        ref[pl.ds(pl.multiple_of(start, 8), size), :] = value

    def basis_stage(s):
        width = WIDTHS[s]
        base = STARTS[s] * 4
        half = width * 2
        xr, zr = half // 4, half // 16
        za = zr // 2
        own = base + core * half
        mine = own + x * xr

        if s == 0:
            loads[0].wait()
            bt_in[...] = b_in[...].T
            loads[1].wait()
            value = dot(bt_in[...], tin[...], ((1,), (1,)))
        else:
            c = STARTS[s] - TOKENS
            value = dot(bt_in[...], qin[:, c:c + width])
        for tile in range(width // LANES):
            pb[base + tile * JB:base + (tile + 1) * JB, :] = value[:, tile * LANES:(tile + 1) * LANES]
        yield

        landing = ls.at[pl.ds(base // 2, half)]
        pair = send(rows(pb, base + (1 - core) * half, half), landing, sibling)
        yield

        pair.wait_recv()
        put(pb, own, half, get(pb, own, half) + ls[base // 2:base // 2 + half, :])
        lxo = base // 8
        sent = [
            send(rows(pb, own + ((x + d) % 4) * xr, xr), lx.at[d - 1, pl.ds(lxo, xr)], xs[d])
            for d in (2, 1, 3)
        ]
        yield

        for one in sent:
            one.wait_recv()
        put(pb, mine, xr, get(pb, mine, xr) + lx[0, lxo:lxo + xr, :]
            + lx[1, lxo:lxo + xr, :] + lx[2, lxo:lxo + xr, :])
        zo = base // 64

        def piece(p, second=0):
            return mine + ((zh + p) % 4) * zr + second * za

        def zland(ref, n):
            return ref.at[n, pl.ds(zo, za)]

        far_a = send(rows(pb, piece(2), za), zland(lz, 0), zhs[1])
        far_b = send(rows(pb, piece(2, 1), za), zland(lz, 2), zhs[3])
        near_b = send(rows(pb, piece(1, 1), za), zland(lz, 1), zhs[1])
        near_a = send(rows(pb, piece(3), za), zland(lz, 3), zhs[3])
        yield

        far_a.wait_recv()
        cz[0, zo:zo + za, :] = lz[0, zo:zo + za, :] + get(pb, piece(1), za)
        sum_a = send(zland(cz, 0), zland(lw, 0), zhs[1])
        far_b.wait_recv()
        cz[1, zo:zo + za, :] = lz[2, zo:zo + za, :] + get(pb, piece(3, 1), za)
        sum_b = send(zland(cz, 1), zland(lw, 1), zhs[3])
        yield

        near_a.wait_recv()
        near_b.wait_recv()
        sum_a.wait_recv()
        put(fb, piece(0), za, get(pb, piece(0), za) + lw[0, zo:zo + za, :] + lz[3, zo:zo + za, :])
        sum_b.wait_recv()
        put(fb, piece(0, 1), za, get(pb, piece(0, 1), za) + lw[1, zo:zo + za, :] + lz[1, zo:zo + za, :])
        up = send(rows(fb, piece(0), zr), rows(fb, piece(0), zr), zhs[1])
        down = send(rows(fb, piece(0), zr), rows(fb, piece(0), zr), zhs[3])
        yield

        up.wait_recv()
        up2 = send(rows(fb, piece(3), za), rows(fb, piece(3), za), zhs[1])
        down.wait_recv()
        down2 = send(rows(fb, piece(1, 1), za), rows(fb, piece(1, 1), za), zhs[3])
        yield

        up2.wait_recv()
        down2.wait_recv()
        sent = [send(rows(fb, mine, xr), rows(fb, mine, xr), xs[d]) for d in (2, 1, 3)]
        yield

        for one in sent:
            one.wait_recv()
        across = send(rows(fb, own, half), rows(fb, own, half), sibling)
        yield

        across.wait_recv()

    def query_stage(s):
        width = WIDTHS[s]
        base = STARTS[s] * 2
        yr = width // 2
        mine = base + y * yr

        if s == 0:
            loads[2].wait()
            bt_out[...] = b_out[...].T
            loads[3].wait()
            value = dot(bt_out[...], tgr[...], ((1,), (1,)))
        else:
            c = STARTS[s] - TOKENS
            value = dot(bt_out[...], qout[:, c:c + width])
        for tile in range(width // LANES):
            pq[base + tile * IB:base + (tile + 1) * IB, :] = value[:, tile * LANES:(tile + 1) * LANES]
        yield

        lyo = base // 4
        sent = [
            send(rows(pq, base + ((y + d) % 4) * yr, yr), ly.at[d - 1, pl.ds(lyo, yr)], ys[d])
            for d in (2, 1, 3)
        ]
        yield

        for one in sent:
            one.wait_recv()
        put(pq, mine, yr, get(pq, mine, yr) + ly[0, lyo:lyo + yr, :]
            + ly[1, lyo:lyo + yr, :] + ly[2, lyo:lyo + yr, :])
        end = jnp.logical_or(zl == 0, zl == 3)
        middle = jnp.logical_or(zl == 1, zl == 2)
        inward = dev(zl=jnp.where(zl == 0, 1, 2))
        outward = dev(zl=jnp.where(zl == 1, 0, 3))
        over = dev(zl=3 - zl)
        block = rows(pq, mine, yr)
        done = rows(fq, mine, yr)
        to_middle = copy(block, le.at[pl.ds(lyo, yr)], inward)
        swap = copy(block, li.at[pl.ds(lyo, yr)], over)
        to_end = copy(done, done, outward)

        def when_sent(condition, one):
            def wait():
                @pl.when(condition)
                def _():
                    one.wait_send()

            unsent.append((tick[0], wait))

        @pl.when(end)
        def _():
            to_middle.start()

        when_sent(end, to_middle)
        yield

        @pl.when(middle)
        def _():
            to_middle.wait_recv()
            put(pq, mine, yr, get(pq, mine, yr) + le[lyo:lyo + yr, :])
            swap.start()

        when_sent(middle, swap)
        yield

        @pl.when(middle)
        def _():
            swap.wait_recv()
            put(fq, mine, yr, get(pq, mine, yr) + li[lyo:lyo + yr, :])
            to_end.start()

        when_sent(middle, to_end)
        yield

        @pl.when(end)
        def _():
            to_end.wait_recv()

        sent = [send(done, done, ys[d]) for d in (2, 1, 3)]
        yield

        for one in sent:
            one.wait_recv()

    def tiles(ref, base, count, size):
        return jnp.concatenate([ref[base + n * size:base + (n + 1) * size, :] for n in range(count)], axis=1)

    store_total = pltpu.make_async_copy(total_bf, o_total, load_sem.at[9])

    def make_scaled():
        g = tiles(fq, 0, 2, IB)
        a_hi, a_lo = split(tiles(fb, 0, 2, JB))
        g_hi, g_lo = split(g)
        loads[7].wait()
        zero = jnp.zeros_like(g_hi)
        total = None
        nt = ((1,), (1,))
        for n in range(EXAMPLES):
            mask = jnp.broadcast_to(eid[...] == n, (IB, TOKENS))
            high, low = jnp.where(mask, g_hi, zero), jnp.where(mask, g_lo, zero)
            scaled = (dot(high, a_hi, nt) + dot(high, a_lo, nt) + dot(low, a_hi, nt)) * inv[...]
            total = scaled if total is None else total + scaled
            hi, lo = split(scaled)
            s_hi[n] = hi
            s_lo[n] = lo
        total_bf[...] = total.astype(jnp.bfloat16)
        store_total.start()

    def influence_of(s):
        width = WIDTHS[s]
        c = STARTS[s] - TOKENS
        count = width // LANES
        for first in range(0, count, 2):
            many = min(2, count - first)
            r_hi, r_lo = split(tiles(fb, STARTS[s] * 4 + first * JB, many, JB))
            out = tiles(fq, STARTS[s] * 2 + first * IB, many, IB)
            at = c + first * LANES
            for n in range(EXAMPLES):
                weighted = dot(s_hi[n], r_hi) + dot(s_hi[n], r_lo) + dot(s_lo[n], r_hi)
                part[n:n + 1, at:at + many * LANES] = jnp.sum(weighted * out, axis=0, keepdims=True)

    part[...] = jnp.zeros_like(part)
    chains = [[basis_stage(s) for s in range(STAGES)], [query_stage(s) for s in range(STAGES)]]
    next(chains[0][0])
    next(chains[1][0])
    pl.semaphore_wait(barrier, len(peers))
    next(chains[0][0])
    next(chains[1][0])
    loads[4].wait()
    loads[5].wait()
    for s in range(1, STAGES):
        next(chains[0][s])
        next(chains[1][s])
    steps = list(ORDER)
    steps.remove((0, 0))
    steps.remove((1, 0))
    for kind, s in steps:
        if kind < 2:
            next(chains[kind][s], None)
        elif s == 0:
            loads[6].wait()
            inv[...] = 1.0 / (eig[...] + DAMPING)
            make_scaled()
            lane = lax.broadcasted_iota(jnp.int32, (QC, LANES), 1)
            row = lax.broadcasted_iota(jnp.int32, (QC, LANES), 0)
            chosen[...] = (row // RANK == lane).astype(jnp.bfloat16)
        else:
            influence_of(s)
        tick[0] += 1
        drain(tick[0] - 16)

    value = select_dot(part[...], chosen[...])

    def reduce(value, slots, index, targets):
        slots[index] = value
        sent = [send(slots.at[index], slots.at[index], target) for target in targets]
        for one in sent:
            one.wait_recv()
        total = slots[0]
        for n in range(1, slots.shape[0]):
            total = total + slots[n]
        return total

    value = reduce(value, ar_c, core, [sibling])
    value = reduce(value, ar_p, x * 4 + y, plane)
    value = reduce(value, ar_z, z, column)

    loads[8].wait()
    task = lax.broadcasted_iota(jnp.int32, (TASKS, QUERIES), 0)
    table = (jnp.broadcast_to(tid[...], (TASKS, QUERIES)) == task).astype(jnp.bfloat16)
    nt = ((1,), (1,))
    counts = dot(jnp.ones((8, QUERIES), jnp.bfloat16), table, nt)
    tasks = select_dot(value[:, :QUERIES], table, nt)
    o_inf[...] = value[:EXAMPLES, :QUERIES]
    o_task[...] = tasks[:EXAMPLES] / counts[:EXAMPLES]
    drain(tick[0] + 1)
    store_total.wait()


def finish(*refs):
    for src, dst in zip(refs[:3], refs[3:]):
        dst[...] = src[...]


def shards(train_inputs, train_grads, example_ids, task_ids, basis_in, basis_out, eigenvalues, query_in, query_out):
    vm = pltpu.VMEM
    f32, bf16 = jnp.float32, jnp.bfloat16
    example_ids = example_ids.reshape(1, TOKENS)
    task_ids = task_ids.reshape(1, QUERIES)
    loaded = [
        vm(a.shape, a.dtype)
        for a in (train_inputs, train_grads, example_ids, task_ids, basis_in, basis_out, eigenvalues, query_in, query_out)
    ]
    scratch = loaded + [
        vm((JB, IB), bf16),
        vm((IB, JB), bf16),
        vm((IB, JB), f32),
        vm((IB, JB), bf16),
        vm((QC, LANES), bf16),
        vm((TOTAL * 4, LANES), f32),
        vm((TOTAL * 4, LANES), f32),
        vm((TOTAL * 2, LANES), f32),
        vm((3, TOTAL // 2, LANES), f32),
        vm((4, TOTAL // 16, LANES), f32),
        vm((2, TOTAL // 16, LANES), f32),
        vm((2, TOTAL // 16, LANES), f32),
        vm((TOTAL * 2, LANES), f32),
        vm((TOTAL * 2, LANES), f32),
        vm((3, TOTAL // 2, LANES), f32),
        vm((TOTAL // 2, LANES), f32),
        vm((TOTAL // 2, LANES), f32),
        vm((EXAMPLES, IB, JB), bf16),
        vm((EXAMPLES, IB, JB), bf16),
        vm((8, QC), f32),
        vm((2, 8, LANES), f32),
        vm((16, 8, LANES), f32),
        vm((16, 8, LANES), f32),
        pltpu.SemaphoreType.DMA((COPIES,)),
        pltpu.SemaphoreType.DMA((COPIES,)),
        pltpu.SemaphoreType.DMA((10,)),
    ]
    shapes = (
        jax.ShapeDtypeStruct((IB, JB), bf16),
        jax.ShapeDtypeStruct((EXAMPLES, QUERIES), f32),
        jax.ShapeDtypeStruct((EXAMPLES, TASKS), f32),
    )
    results = pl.pallas_call(
        kernel,
        out_shape=shapes,
        in_specs=[pl.BlockSpec(memory_space=pl.ANY)] * 9,
        out_specs=[pl.BlockSpec(memory_space=pl.ANY)] + [pl.BlockSpec(memory_space=pltpu.VMEM)] * 2,
        scratch_shapes=scratch,
        compiler_params=pltpu.CompilerParams(
            collective_id=0, has_side_effects=True, vmem_limit_bytes=62 * 2**20
        ),
        name="influence",
    )(train_inputs, train_grads, example_ids, task_ids, basis_in, basis_out, eigenvalues, query_in, query_out)
    return pl.pallas_call(
        finish,
        out_shape=shapes,
        in_specs=[pl.BlockSpec(memory_space=pltpu.VMEM)] * 3,
        out_specs=[pl.BlockSpec(memory_space=pltpu.VMEM)] * 3,
        compiler_params=pltpu.CompilerParams(vmem_limit_bytes=62 * 2**20),
        name="finish",
    )(*results)


def solution(mesh):
    in_specs = (
        P(None, "basis"),
        P(None, "query"),
        P(),
        P(),
        P("basis", "query"),
        P("query", "basis"),
        P("basis", "query"),
        P("basis", None),
        P("query", None),
    )
    out_specs = (P("basis", "query"), P(), P())
    return jax.shard_map(shards, mesh=mesh, in_specs=in_specs, out_specs=out_specs, check_vma=False)
```
